512 devices in a mesh: ctx: 16 (over z), beam: 32 (over y, x, core).
Axes of the slice: x: 4, y: 4, z: 16, core: 2. Of those that a mesh axis runs over, the one named last changes fastest.
Arguments:
- queries: bfloat16 [512, 64, 128], P('beam', 'ctx'), may hold values from -20 to 20
- prompt_kv: bfloat16 [2, 16384, 8, 128], P(None, 'ctx'), may hold values from -16 to 16
- suffix_kv: bfloat16 [2, 512, 64, 8, 128], P(None, 'beam', 'ctx'), may hold values from -9 to 9
- new_kv: bfloat16 [2, 512, 8, 128], P(None, 'beam'), may hold values from -11 to 11
- parents: int32 [512], P('beam'), may hold values from 0 to 511, as said below
- lengths: int32 [512], P('beam'), may hold values from 1 to 64, as said below
- token_ids: int32 [512], P('beam'), may hold values from 0 to 128255
- group_ids: int32 [512], P('beam'), may hold values from 0 to 7
Outputs:
- attended: bfloat16 [512, 64, 128], P('beam', 'ctx')
- penalty: float32 [512], P('beam')
The draws below stay inside these ranges and needn't reach their ends.
Inputs may be any that keep to these rules, and one draw needn't show every extreme that they name: parents[b] lies in the same aligned block of 64 beams as b. `lengths`: some beam has exactly 64 live suffix positions and some exactly 1.
All inputs are finite; a program needn't handle non-finite values.
Results may differ from the reference program's by a relative error of at most 0.014.
Values may be sent and summed in bfloat16 or wider, within the bound.
No kernel may reach another device: no remote copies, remote signals or barrier semaphores. Data moves between devices by JAX's collectives and lax.ppermute only.
A program may use at most 64 MiB of HBM per device.

```python
import math
import jax
import jax.numpy as jnp
import numpy as np
from jax import lax

HEADS = 64
KVH = 8
HD = 128
VOCAB = 128256
GROUPS = 8
BEAMS = 512
FAMILY = 64
PROMPT = 16384
SUF = 64


def family_direction(key):
    return jnp.clip(jax.random.normal(jax.random.fold_in(key, 7), (BEAMS // FAMILY, KVH, HD), jnp.float32), -4.0, 4.0)


def family_of_beams(key):
    return jnp.repeat(family_direction(key), FAMILY, axis=0)


def base_queries(key):
    noise = jnp.clip(jax.random.normal(jax.random.fold_in(key, 8), (BEAMS, HEADS, HD), jnp.float32), -4.0, 4.0)
    shared = jnp.repeat(family_of_beams(key), HEADS // KVH, axis=1)
    return 0.8 * shared + 0.6 * noise


def draw_queries(key, part):
    base = base_queries(key)
    return base.astype(jnp.bfloat16)


def draw_prompt_kv(key, part):
    key = jax.random.fold_in(key, 12)
    keys_part = 2.5 * jnp.clip(jax.random.normal(jax.random.fold_in(key, 1), (PROMPT, KVH, HD), jnp.float32), -6.0, 6.0)
    values_part = jnp.clip(jax.random.normal(jax.random.fold_in(key, 2), (PROMPT, KVH, HD), jnp.float32), -6.0, 6.0)
    return jnp.stack((keys_part, values_part)).astype(jnp.bfloat16)


def draw_suffix_kv(key, part):
    shared = family_of_beams(key)
    key = jax.random.fold_in(key, 13)
    noise = jnp.clip(jax.random.normal(jax.random.fold_in(key, 1), (BEAMS, SUF, KVH, HD), jnp.float32), -6.0, 6.0)
    keys_part = 0.7 * shared[:, None, :, :] + noise
    values_part = jnp.clip(jax.random.normal(jax.random.fold_in(key, 2), (BEAMS, SUF, KVH, HD), jnp.float32), -6.0, 6.0)
    return jnp.stack((keys_part, values_part)).astype(jnp.bfloat16)


def draw_new_kv(key, part):
    shared = family_of_beams(key)
    key = jax.random.fold_in(key, 14)
    noise = jnp.clip(jax.random.normal(jax.random.fold_in(key, 1), (BEAMS, KVH, HD), jnp.float32), -6.0, 6.0)
    keys_part = 1.1 * shared + noise
    values_part = jnp.clip(jax.random.normal(jax.random.fold_in(key, 2), (BEAMS, KVH, HD), jnp.float32), -6.0, 6.0)
    return jnp.stack((keys_part, values_part)).astype(jnp.bfloat16)


def draw_parents(key, part):
    key = jax.random.fold_in(key, 21)
    offset = jax.random.randint(key, (BEAMS,), 0, FAMILY)
    return (jnp.arange(BEAMS, dtype=jnp.int32) // FAMILY * FAMILY + offset).astype(jnp.int32)


def draw_lengths(key, part):
    key = jax.random.fold_in(key, 31)
    drawn_lengths = jax.random.randint(jax.random.fold_in(key, 1), (BEAMS,), 1, SUF + 1)
    longest = jax.random.randint(jax.random.fold_in(key, 2), (), 0, BEAMS)
    beam_numbers = jnp.arange(BEAMS, dtype=jnp.int32)
    drawn_lengths = jnp.where(beam_numbers == longest, SUF, drawn_lengths)
    drawn_lengths = jnp.where(beam_numbers == (longest + 1) % BEAMS, 1, drawn_lengths)
    return drawn_lengths.astype(jnp.int32)


def place_ends(result, rng, smallest, top_value):
    shape = result.shape
    index_at = [jax.random.randint(jax.random.fold_in(rng, axis), (), 0, shape[axis]) for axis in range(len(shape))]
    result = result.at[tuple(index_at)].set(smallest)
    longest = shape.index(max(shape))
    index_at[longest] = (index_at[longest] + 1) % shape[longest]
    return result.at[tuple(index_at)].set(top_value)


def wide_ids(rng, extent, count, skew):
    weights = [min(1 << octave, count + 1 - (1 << octave)) * (1 << 20) // math.isqrt((1 << octave) ** skew) + 1 for octave in range((count + 1).bit_length()) if 1 << octave <= count]
    scale = 1 + sum(weights) // (1 << 30)
    listing = np.cumsum(np.array([max(1, weight // scale) for weight in weights]))
    ticket = jax.random.randint(jax.random.fold_in(rng, 1), extent, 0, int(listing[len(weights) - 1]))
    start = jnp.left_shift(1, jnp.searchsorted(jnp.asarray(listing, jnp.int32), ticket, side="right").astype(jnp.int32))
    standing = start - 1 + jax.random.randint(jax.random.fold_in(rng, 4), extent, 0, 1 << 30) % jnp.minimum(start, count + 1 - start)
    return jax.random.permutation(jax.random.fold_in(rng, 2), count)[standing].astype(jnp.int32)


def setup_inputs(seed: int = 0) -> dict:
    key_list = jax.random.split(jax.random.key(seed), 9)
    return {
        "queries": draw_queries(jax.random.fold_in(key_list[8], 71), 0),
        "prompt_kv": draw_prompt_kv(jax.random.fold_in(key_list[8], 71), 0),
        "suffix_kv": draw_suffix_kv(jax.random.fold_in(key_list[8], 71), 0),
        "new_kv": draw_new_kv(jax.random.fold_in(key_list[8], 71), 0),
        "parents": draw_parents(jax.random.fold_in(key_list[8], 71), 0),
        "lengths": draw_lengths(jax.random.fold_in(key_list[8], 71), 0),
        "token_ids": place_ends(wide_ids(key_list[6], (BEAMS,), VOCAB, 4), jax.random.fold_in(key_list[6], 3), 0, VOCAB - 1).astype(jnp.int32),
        "group_ids": place_ends(jax.random.randint(key_list[7], (BEAMS,), 0, GROUPS), jax.random.fold_in(key_list[7], 1), 0, GROUPS - 1).astype(jnp.int32),
    }


PENALTY_WEIGHT = 0.5


def rounded_weights(weights):
    return lax.optimization_barrier(weights.astype(jnp.bfloat16)).astype(jnp.float32)


def reference(queries, prompt_kv, suffix_kv, new_kv, parents, lengths, token_ids, group_ids):
    group_size = HEADS // KVH
    score_scale = HD ** -0.5
    prompt_keys = prompt_kv[0].astype(jnp.float32)
    prompt_values = prompt_kv[1].astype(jnp.float32)
    reordered = jnp.take(suffix_kv, parents, axis=1)
    positions = jnp.arange(SUF, dtype=jnp.int32)
    per_beam = (queries, jnp.moveaxis(reordered, 1, 0), jnp.moveaxis(new_kv, 1, 0), lengths)

    def one_beam(entries):
        query, suffix, own_kv, length = entries
        query_group = query.astype(jnp.float32).reshape(KVH, group_size, HD)
        s_prompt = jnp.einsum('kgd,pkd->kgp', query_group, prompt_keys) * score_scale
        s_suffix = jnp.einsum('kgd,skd->kgs', query_group, suffix[0].astype(jnp.float32)) * score_scale
        s_suffix = jnp.where(positions[None, None, :] < length, s_suffix, -jnp.inf)
        s_own = jnp.einsum('kgd,kd->kg', query_group, own_kv[0].astype(jnp.float32)) * score_scale
        ceiling = jnp.maximum(jnp.maximum(jnp.max(s_prompt, axis=2), jnp.max(s_suffix, axis=2)), s_own)
        prompt_weights = jnp.exp(s_prompt - ceiling[..., None])
        suffix_weights = jnp.exp(s_suffix - ceiling[..., None])
        own_weights = jnp.exp(s_own - ceiling)
        running_totals = jnp.sum(prompt_weights, axis=2) + jnp.sum(suffix_weights, axis=2) + own_weights
        mixed = jnp.einsum('kgp,pkd->kgd', rounded_weights(prompt_weights), prompt_values)
        mixed = mixed + jnp.einsum('kgs,skd->kgd', rounded_weights(suffix_weights), suffix[1].astype(jnp.float32))
        mixed = mixed + jnp.einsum('kg,kd->kgd', rounded_weights(own_weights), own_kv[1].astype(jnp.float32))
        return (mixed / running_totals[..., None]).reshape(HEADS, HD).astype(jnp.bfloat16)

    attended = lax.map(one_beam, per_beam)
    earlier = (group_ids[None, :] < group_ids[:, None]) & (token_ids[None, :] == token_ids[:, None])
    penalty = PENALTY_WEIGHT * jnp.sum(earlier.astype(jnp.float32), axis=1)
    return attended, penalty
```

```python
import functools

import jax
import jax.numpy as jnp
from jax import lax
from jax.experimental import pallas as pl
from jax.experimental.pallas import tpu as pltpu
from jax.sharding import PartitionSpec as P

HEADS = 64
KVH = 8
HD = 128
FAMILY_DEVICES = 4
PENALTY_WEIGHT = 0.5
FAR_BELOW = -1e30
LOG2E = 1.4426950408889634
EXTRA = 16


def rows_by_head(count):
    row = lax.broadcasted_iota(jnp.int32, (128, 128), 0)
    col = lax.broadcasted_iota(jnp.int32, (128, 128), 1)
    per = 128 // count
    hit = (row // per == col % count) & (row % per == col // count)
    return jnp.where(hit, 1.0, 0.0).astype(jnp.bfloat16)


def attend_kernel(parents, lengths, q_ref, kv_ref, s0, s1, s2, s3, new_ref, out_ref, picked, ext):
    beams = 16
    z = lax.axis_index("ctx")
    place = lax.axis_index("beam") % FAMILY_DEVICES
    scale = HD**-0.5

    for b in range(beams):
        parent = parents[b]
        slot = lax.bitwise_xor((parent // beams) % FAMILY_DEVICES, place)
        local = parent % beams
        for k, held in enumerate((s0, s1, s2, s3)):

            @pl.when(slot == k)
            def _(held=held, local=local, b=b):
                for c in range(2):
                    picked[c, pl.ds(b * 32, 32)] = held[c, local]

    by_head = rows_by_head(KVH)
    ext[...] = jnp.zeros_like(ext)
    for c in range(2):
        for part in range(5):
            rows = picked[c, pl.ds(part * 128, 128)] if part < 4 else new_ref[c]
            moved = jnp.dot(by_head, rows, preferred_element_type=jnp.float32).astype(jnp.bfloat16)
            for g in range(KVH):
                ext[c, g, pl.ds(part * 16, 16)] = moved[g * 16 : (g + 1) * 16]

    row = lax.broadcasted_iota(jnp.int32, (128, 128), 0)
    col = lax.broadcasted_iota(jnp.int32, (128, 128), 1)
    row_beam = (row % 64) // 4
    live = jnp.zeros((128, 128), jnp.int32)
    for b in range(beams):
        live = jnp.where(row_beam == b, lengths[b], live)
    on_suffix = (col < 64) & (col // 4 == row_beam) & (z * 4 + col % 4 < live)
    on_new = (col >= 64) & (col - 64 == row_beam)
    bias_plain = jnp.where(on_suffix, 0.0, FAR_BELOW)
    bias_new = jnp.where(on_suffix | on_new, 0.0, FAR_BELOW)

    transposed = (((1,), (1,)), ((), ()))
    stats = jnp.zeros((128, 128), jnp.float32)
    for g in range(KVH):
        q = q_ref[2 * g : 2 * g + 2].reshape(128, HD)
        s = lax.dot_general(q, kv_ref[0, g], transposed, preferred_element_type=jnp.float32)
        e = lax.dot_general(q, ext[0, g], transposed, preferred_element_type=jnp.float32)
        e = e + jnp.where(z == 2 * g, bias_new, bias_plain)
        m = jnp.maximum(jnp.max(s, axis=1, keepdims=True), jnp.max(e, axis=1, keepdims=True))
        p = jnp.exp2((s - m) * (scale * LOG2E))
        pe = jnp.exp2((e - m) * (scale * LOG2E))
        total = jnp.sum(p, axis=1, keepdims=True) + jnp.sum(pe, axis=1, keepdims=True)
        o = jnp.dot(p.astype(jnp.bfloat16), kv_ref[1, g], preferred_element_type=jnp.float32)
        o = o + jnp.dot(pe.astype(jnp.bfloat16), ext[1, g], preferred_element_type=jnp.float32)
        o = (o / total).astype(jnp.bfloat16)
        out_ref[2 * g, 0:64] = o[0:64]
        out_ref[2 * g + 1, 0:64] = o[64:128]
        stats = jnp.where(col == g, m * scale + jnp.log(total), stats)
    flat = stats.T[0:KVH]
    high = flat.astype(jnp.bfloat16).astype(jnp.float32)
    middle = (flat - high).astype(jnp.bfloat16).astype(jnp.float32)
    low = flat - high - middle
    place_row = lax.broadcasted_iota(jnp.int32, (EXTRA, 128), 0)
    for g in range(KVH):
        block = jnp.where(place_row == 0, high[g : g + 1], 0.0)
        block = jnp.where(place_row == 1, middle[g : g + 1], block)
        block = jnp.where(place_row == 2, low[g : g + 1], block).astype(jnp.bfloat16)
        out_ref[2 * g, 64 : 64 + EXTRA] = block
        out_ref[2 * g + 1, 64 : 64 + EXTRA] = block


def combine_kernel(parts_ref, out_ref):
    z = lax.axis_index("ctx")
    extra = parts_ref[:, 64 : 64 + EXTRA].astype(jnp.float32)
    logs = extra[:, 0] + extra[:, 1] + extra[:, 2]
    weights = jnp.exp(logs - jnp.max(logs, axis=0, keepdims=True))
    weights = weights / jnp.sum(weights, axis=0, keepdims=True)
    weights = jnp.where(z % 2 == 1, pltpu.roll(weights, 64, 1), weights)
    by_row = weights.T[0:64]
    mixed = jnp.zeros((64, HD), jnp.float32)
    for source in range(16):
        mixed = mixed + by_row[:, source : source + 1] * parts_ref[source, 0:64].astype(jnp.float32)
    out_ref[...] = mixed.astype(jnp.bfloat16)


def body(queries, prompt_kv, suffix_kv, new_kv, parents, lengths, token_ids, group_ids):
    vmem = pl.BlockSpec(memory_space=pltpu.VMEM)
    smem = pl.BlockSpec(memory_space=pltpu.SMEM)

    own = queries.reshape(1, 64, HD)
    with jax.named_scope("queries_to_all"):
        everyone = lax.all_to_all(
            jnp.broadcast_to(own, (16, 64, HD)), "ctx", 0, 0, tiled=True
        )
    suffix = suffix_kv.reshape(2, 16, 32, HD)
    with jax.named_scope("suffix_family"):
        held = [suffix] + [
            lax.ppermute(suffix, "beam", [(i, i ^ k) for i in range(32)]) for k in (1, 2, 3)
        ]
    by_head = jnp.transpose(prompt_kv, (0, 2, 1, 3))

    parts = pl.pallas_call(
        attend_kernel,
        out_shape=jax.ShapeDtypeStruct((16, 64 + EXTRA, HD), jnp.bfloat16),
        in_specs=[smem, smem] + [vmem] * 7,
        out_specs=vmem,
        scratch_shapes=[
            pltpu.VMEM((2, 512, HD), jnp.bfloat16),
            pltpu.VMEM((2, KVH, 128, HD), jnp.bfloat16),
        ],
        compiler_params=pltpu.CompilerParams(vmem_limit_bytes=32 * 2**20),
        cost_estimate=pl.CostEstimate(
            flops=600_000_000, bytes_accessed=6_000_000, transcendentals=1_200_000
        ),
        name="attend",
    )(parents, lengths, everyone, by_head, *held, new_kv.reshape(2, 128, HD))

    with jax.named_scope("parts_home"):
        parts = lax.all_to_all(parts, "ctx", 0, 0, tiled=True)
    attended = pl.pallas_call(
        combine_kernel,
        out_shape=jax.ShapeDtypeStruct((64, HD), jnp.bfloat16),
        in_specs=[vmem],
        out_specs=vmem,
        name="combine",
    )(parts).reshape(16, 4, HD)

    all_tokens, all_groups = (
        lax.all_gather(token_ids, "beam", axis=0, tiled=True),
        lax.all_gather(group_ids, "beam", axis=0, tiled=True),
    )
    earlier = (all_groups[None, :] < group_ids[:, None]) & (
        all_tokens[None, :] == token_ids[:, None]
    )
    penalty = PENALTY_WEIGHT * jnp.sum(earlier.astype(jnp.float32), axis=1)
    return (attended, penalty)


def solution(mesh):
    in_specs = (
        P("beam", "ctx", None),
        P(None, "ctx", None, None),
        P(None, "beam", "ctx", None, None),
        P(None, "beam", None, None),
        P("beam"),
        P("beam"),
        P("beam"),
        P("beam"),
    )
    out_specs = (P("beam", "ctx", None), P("beam"))
    return jax.shard_map(body, mesh=mesh, in_specs=in_specs, out_specs=out_specs, check_vma=False)
```

```python
import functools

import jax
import jax.numpy as jnp
from jax import lax
from jax.experimental import pallas as pl
from jax.experimental.pallas import tpu as pltpu
from jax.sharding import PartitionSpec as P

HEADS = 64
KVH = 8
HD = 128
FAMILY_DEVICES = 4
PENALTY_WEIGHT = 0.5
FAR_BELOW = -1e30
LOG2E = 1.4426950408889634
EXTRA = 8


def rows_by_head(count):
    row = lax.broadcasted_iota(jnp.int32, (128, 128), 0)
    col = lax.broadcasted_iota(jnp.int32, (128, 128), 1)
    per = 128 // count
    hit = (row // per == col % count) & (row % per == col // count)
    return jnp.where(hit, 1.0, 0.0).astype(jnp.bfloat16)


def by_head_kernel(kv_ref, out_ref, natural, moved, in_sems, out_sems):
    step = 256
    chunks = [(c, pl.ds(first, step)) for c in range(2) for first in range(0, 1024, step)]
    loads = [
        pltpu.make_async_copy(kv_ref.at[c, rows], natural.at[c, rows], in_sems.at[n])
        for n, (c, rows) in enumerate(chunks)
    ]
    stores = [
        pltpu.make_async_copy(moved.at[c, :, rows], out_ref.at[c, :, rows], out_sems.at[n])
        for n, (c, rows) in enumerate(chunks)
    ]
    for load in loads:
        load.start()
    for (c, rows), load, store in zip(chunks, loads, stores):
        load.wait()
        for first in range(0, step, 64):
            part = pl.ds(rows.start + first, 64)
            moved[c, :, part] = jnp.swapaxes(natural[c, part], 0, 1)
        store.start()
    for store in stores:
        store.wait()


def token_rows_kernel(token_ids, group_ids, rows_a, rows_b):
    row = lax.broadcasted_iota(jnp.int32, (EXTRA, 128), 0)
    lane = lax.broadcasted_iota(jnp.int32, (EXTRA, 128), 1)
    for rows_ref, first_lane in ((rows_a, 0), (rows_b, 16)):
        tokens = jnp.zeros((EXTRA, 128), jnp.int32)
        groups = jnp.zeros((EXTRA, 128), jnp.int32)
        for b in range(16):
            tokens = jnp.where(lane == first_lane + b, token_ids[b], tokens)
            groups = jnp.where(lane == first_lane + b, group_ids[b], groups)
        digits = jnp.where(row == 3, tokens >> 16, 0)
        digits = jnp.where(row == 4, (tokens >> 8) & 255, digits)
        digits = jnp.where(row == 5, tokens & 255, digits)
        digits = jnp.where(row == 6, groups, digits)
        rows_ref[...] = digits.astype(jnp.float32).astype(jnp.bfloat16)


def attend_kernel(
    parents_ref, lengths_ref, q_ref, kv_ref, near, far, new_ref, tok_a, tok_b, out_ref,
    kv, picked, ext, new_rows, parents, lengths, sems, small_sems,
):
    beams = 16
    z = lax.axis_index("ctx")
    place = lax.axis_index("beam") % FAMILY_DEVICES
    scale = HD**-0.5

    loads = [
        pltpu.make_async_copy(kv_ref.at[c, g], kv.at[c, g], sems.at[c, g])
        for g in range(KVH)
        for c in range(2)
    ]
    small = [
        pltpu.make_async_copy(source, target, small_sems.at[n])
        for n, (source, target) in enumerate(
            ((parents_ref, parents), (lengths_ref, lengths), (new_ref, new_rows))
        )
    ]
    for load in small + loads:
        load.start()
    for load in small:
        load.wait()

    for b in range(beams):
        parent = parents[b]
        slot = lax.bitwise_xor((parent // beams) % FAMILY_DEVICES, place)
        local = parent % beams
        for k, held in enumerate((near, far)):

            @pl.when(slot % 2 == k)
            def _(held=held, local=local, slot=slot, b=b):
                for c in range(2):
                    picked[c, pl.ds(b * 32, 32)] = held[slot // 2, c, local]

    by_head = rows_by_head(KVH)
    ext[...] = jnp.zeros_like(ext)
    for c in range(2):
        for part in range(5):
            rows = picked[c, pl.ds(part * 128, 128)] if part < 4 else new_rows[c]
            moved = jnp.dot(by_head, rows, preferred_element_type=jnp.float32).astype(jnp.bfloat16)
            for g in range(KVH):
                ext[c, g, pl.ds(part * 16, 16)] = moved[g * 16 : (g + 1) * 16]

    row = lax.broadcasted_iota(jnp.int32, (128, 128), 0)
    col = lax.broadcasted_iota(jnp.int32, (128, 128), 1)
    row_beam = (row % 64) // 4
    live = jnp.zeros((128, 128), jnp.int32)
    for b in range(beams):
        live = jnp.where(row_beam == b, lengths[b], live)
    on_suffix = (col < 64) & (col // 4 == row_beam) & (z * 4 + col % 4 < live)
    on_new = (col >= 64) & (col - 64 == row_beam)
    bias_plain = jnp.where(on_suffix, 0.0, FAR_BELOW)
    bias_new = jnp.where(on_suffix | on_new, 0.0, FAR_BELOW)

    transposed = (((1,), (1,)), ((), ()))
    stats = jnp.zeros((128, 128), jnp.float32)
    for g in range(KVH):
        q = q_ref[2 * g : 2 * g + 2].reshape(128, HD)
        loads[2 * g].wait()
        s = lax.dot_general(q, kv[0, g], transposed, preferred_element_type=jnp.float32)
        e = lax.dot_general(q, ext[0, g], transposed, preferred_element_type=jnp.float32)
        e = e + jnp.where(z == 2 * g, bias_new, bias_plain)
        m = jnp.maximum(jnp.max(s, axis=1, keepdims=True), jnp.max(e, axis=1, keepdims=True))
        p = jnp.exp2((s - m) * (scale * LOG2E))
        pe = jnp.exp2((e - m) * (scale * LOG2E))
        total = jnp.sum(p, axis=1, keepdims=True) + jnp.sum(pe, axis=1, keepdims=True)
        loads[2 * g + 1].wait()
        o = jnp.dot(p.astype(jnp.bfloat16), kv[1, g], preferred_element_type=jnp.float32)
        o = o + jnp.dot(pe.astype(jnp.bfloat16), ext[1, g], preferred_element_type=jnp.float32)
        o = (o / total).astype(jnp.bfloat16)
        out_ref[2 * g, 0:64] = o[0:64]
        out_ref[2 * g + 1, 0:64] = o[64:128]
        stats = jnp.where(col == g, m * scale + jnp.log(total), stats)
    flat = stats.T[0:KVH]
    high = flat.astype(jnp.bfloat16).astype(jnp.float32)
    middle = (flat - high).astype(jnp.bfloat16).astype(jnp.float32)
    low = flat - high - middle
    place_row = lax.broadcasted_iota(jnp.int32, (EXTRA, 128), 0)
    tokens = tok_a[...].astype(jnp.float32) + tok_b[...].astype(jnp.float32)
    for g in range(KVH):
        block = jnp.where(place_row == 0, high[g : g + 1], tokens)
        block = jnp.where(place_row == 1, middle[g : g + 1], block)
        block = jnp.where(place_row == 2, low[g : g + 1], block).astype(jnp.bfloat16)
        out_ref[2 * g, 64 : 64 + EXTRA] = block
        out_ref[2 * g + 1, 64 : 64 + EXTRA] = block


def combine_kernel(token_ids, group_ids, parts_ref, out_ref, penalty_ref):
    z = lax.axis_index("ctx")
    extra = parts_ref[:, 64 : 64 + EXTRA].astype(jnp.float32)
    logs = extra[:, 0] + extra[:, 1] + extra[:, 2]
    weights = jnp.exp(logs - jnp.max(logs, axis=0, keepdims=True))
    weights = weights / jnp.sum(weights, axis=0, keepdims=True)
    weights = jnp.where(z % 2 == 1, pltpu.roll(weights, 64, 1), weights)
    by_row = weights.T[0:64]
    mixed = jnp.zeros((64, HD), jnp.float32)
    for source in range(16):
        mixed = mixed + by_row[:, source : source + 1] * parts_ref[source, 0:64].astype(jnp.float32)
    out_ref[...] = mixed.astype(jnp.bfloat16)

    all_tokens = extra[:, 3] * 65536.0 + extra[:, 4] * 256.0 + extra[:, 5]
    all_groups = extra[:, 6]
    used = lax.broadcasted_iota(jnp.int32, (16, 128), 1) < 32
    beam = lax.broadcasted_iota(jnp.int32, (16, 128), 0)
    counts = jnp.zeros((16, 128), jnp.float32)
    for b in range(16):
        token = token_ids[b].astype(jnp.float32)
        group = group_ids[b].astype(jnp.float32)
        same = used & (all_tokens == token) & (all_groups < group)
        count = jnp.sum(jnp.where(same, PENALTY_WEIGHT, 0.0), axis=0, keepdims=True)
        counts = jnp.where(beam == b, count, counts)
    penalty_ref[...] = jnp.sum(counts.T, axis=0, keepdims=True)


def within_plane(block, flip):
    pairs = [(z * 32 + b, z * 32 + (b ^ (2 * z) ^ flip)) for z in range(16) for b in range(32)]
    return lax.ppermute(block, ("ctx", "beam"), pairs)


def body(queries, prompt_kv, suffix_kv, new_kv, parents, lengths, token_ids, group_ids):
    vmem = pl.BlockSpec(memory_space=pltpu.VMEM)
    smem = pl.BlockSpec(memory_space=pltpu.SMEM)
    hbm = pl.BlockSpec(memory_space=pl.ANY)

    suffix = suffix_kv.reshape(1, 2, 16, 32, HD)
    with jax.named_scope("suffix_x"):
        across = lax.ppermute(suffix, "beam", [(i, i ^ 2) for i in range(32)])
    own = queries.reshape(1, 64, HD)
    with jax.named_scope("queries_to_all"):
        everyone = lax.all_to_all(
            jnp.broadcast_to(own, (16, 64, HD)), "ctx", 0, 0, tiled=True
        )
    rows_a, rows_b = pl.pallas_call(
        token_rows_kernel,
        out_shape=(jax.ShapeDtypeStruct((EXTRA, 128), jnp.bfloat16),) * 2,
        in_specs=[smem, smem],
        out_specs=(vmem, vmem),
        compiler_params=pltpu.CompilerParams(vmem_limit_bytes=2**20),
        name="token_rows",
    )(token_ids, group_ids)
    by_head = pl.pallas_call(
        by_head_kernel,
        out_shape=jax.ShapeDtypeStruct((12, KVH, 1024, HD), jnp.bfloat16),
        in_specs=[hbm],
        out_specs=hbm,
        scratch_shapes=[
            pltpu.VMEM((2, 1024, KVH, HD), jnp.bfloat16),
            pltpu.VMEM((2, KVH, 1024, HD), jnp.bfloat16),
            pltpu.SemaphoreType.DMA((8,)),
            pltpu.SemaphoreType.DMA((8,)),
        ],
        compiler_params=pltpu.CompilerParams(vmem_limit_bytes=57 * 2**20),
        cost_estimate=pl.CostEstimate(flops=0, bytes_accessed=8_000_000, transcendentals=0),
        name="prompt_by_head",
    )(prompt_kv)
    with jax.named_scope("tokens_plane"):
        tok_a = within_plane(rows_a, 0)
        tok_b = within_plane(rows_b, 1)
    with jax.named_scope("suffix_core"):
        across, by_head, *_ = lax.optimization_barrier((across, by_head, rows_a, rows_b))
        near = jnp.concatenate((suffix, across))
        far = lax.ppermute(near, "beam", [(i, i ^ 1) for i in range(32)])

    parts = pl.pallas_call(
        attend_kernel,
        out_shape=jax.ShapeDtypeStruct((16, 64 + EXTRA, HD), jnp.bfloat16),
        in_specs=[hbm, hbm, vmem, hbm, vmem, vmem, hbm, vmem, vmem],
        out_specs=vmem,
        scratch_shapes=[
            pltpu.VMEM((2, KVH, 1024, HD), jnp.bfloat16),
            pltpu.VMEM((2, 512, HD), jnp.bfloat16),
            pltpu.VMEM((2, KVH, 128, HD), jnp.bfloat16),
            pltpu.VMEM((2, 128, HD), jnp.bfloat16),
            pltpu.SMEM((16,), jnp.int32),
            pltpu.SMEM((16,), jnp.int32),
            pltpu.SemaphoreType.DMA((2, KVH)),
            pltpu.SemaphoreType.DMA((3,)),
        ],
        compiler_params=pltpu.CompilerParams(vmem_limit_bytes=40 * 2**20),
        cost_estimate=pl.CostEstimate(
            flops=600_000_000, bytes_accessed=6_000_000, transcendentals=1_200_000
        ),
        name="attend",
    )(parents, lengths, everyone, by_head, near, far, new_kv.reshape(2, 128, HD), tok_a, tok_b)

    with jax.named_scope("parts_home"):
        parts = lax.all_to_all(parts, "ctx", 0, 0, tiled=True)
    attended, penalty = pl.pallas_call(
        combine_kernel,
        out_shape=(
            jax.ShapeDtypeStruct((64, HD), jnp.bfloat16),
            jax.ShapeDtypeStruct((1, 16), jnp.float32),
        ),
        in_specs=[smem, smem, vmem],
        out_specs=(vmem, vmem),
        compiler_params=pltpu.CompilerParams(vmem_limit_bytes=4 * 2**20),
        name="combine",
    )(token_ids, group_ids, parts)
    return (attended.reshape(16, 4, HD), penalty.reshape(16))


def solution(mesh):
    in_specs = (
        P("beam", "ctx", None),
        P(None, "ctx", None, None),
        P(None, "beam", "ctx", None, None),
        P(None, "beam", None, None),
        P("beam"),
        P("beam"),
        P("beam"),
        P("beam"),
    )
    out_specs = (P("beam", "ctx", None), P("beam"))
    return jax.shard_map(body, mesh=mesh, in_specs=in_specs, out_specs=out_specs, check_vma=False)
```

```python
import jax
import jax.numpy as jnp
from jax import lax
from jax.experimental import pallas as pl
from jax.experimental.pallas import tpu as pltpu
from jax.sharding import PartitionSpec as P

HEADS = 64
KVH = 8
HD = 128
FAMILY_DEVICES = 4
PENALTY_WEIGHT = 0.5
FAR_BELOW = -1e30
LOG2E = 1.4426950408889634
EXTRA = 8


def rows_by_head():
    row = lax.broadcasted_iota(jnp.int32, (128, 128), 0)
    col = lax.broadcasted_iota(jnp.int32, (128, 128), 1)
    hit = (row // 16 == col % KVH) & (row % 16 == col // KVH)
    return jnp.where(hit, 1.0, 0.0).astype(jnp.bfloat16)


def token_rows_kernel(scalars, rows_a, rows_b):
    row = lax.broadcasted_iota(jnp.int32, (EXTRA, 128), 0)
    lane = lax.broadcasted_iota(jnp.int32, (EXTRA, 128), 1)
    for rows_ref, first_lane in ((rows_a, 0), (rows_b, 16)):
        tokens = jnp.zeros((EXTRA, 128), jnp.int32)
        groups = jnp.zeros((EXTRA, 128), jnp.int32)
        for b in range(16):
            tokens = jnp.where(lane == first_lane + b, scalars[b], tokens)
            groups = jnp.where(lane == first_lane + b, scalars[16 + b], groups)
        digits = jnp.where(row == 3, tokens >> 16, 0)
        digits = jnp.where(row == 4, (tokens >> 8) & 255, digits)
        digits = jnp.where(row == 5, tokens & 255, digits)
        digits = jnp.where(row == 6, groups, digits)
        digits = jnp.concatenate((digits, jnp.zeros_like(digits)))
        rows_ref[...] = digits.astype(jnp.float32).astype(jnp.bfloat16)


def prepare_kernel(scalars, new_ref, new_rows_ref, bias_ref):
    z = lax.axis_index("ctx")
    by_head = rows_by_head()
    for c in range(2):
        moved = jnp.dot(by_head, new_ref[c], preferred_element_type=jnp.float32)
        new_rows_ref[c] = moved.astype(jnp.bfloat16)

    row = lax.broadcasted_iota(jnp.int32, (128, 128), 0)
    col = lax.broadcasted_iota(jnp.int32, (128, 128), 1)
    row_beam = (row % 64) // 4
    live = jnp.zeros((128, 128), jnp.int32)
    for b in range(16):
        live = jnp.where(row_beam == b, scalars[32 + b], live)
    on_suffix = (col < 64) & (col // 4 == row_beam) & (z * 4 + col % 4 < live)
    on_new = (col >= 64) & (col - 64 == row_beam)
    bias_ref[0] = jnp.where(on_suffix, 0.0, FAR_BELOW)
    bias_ref[1] = jnp.where(on_suffix | on_new, 0.0, FAR_BELOW)


def attend_kernel(
    scalars, q_ref, kv_ref, near, far, new_rows, bias_ref, out_ref,
    natural, kv, picked, ext, sems,
):
    beams = 16
    z = lax.axis_index("ctx")
    place = lax.axis_index("beam") % FAMILY_DEVICES
    scale = HD**-0.5

    step = 256
    chunks = [(c, pl.ds(first, step)) for c in range(2) for first in range(0, 1024, step)]
    loads = [
        pltpu.make_async_copy(kv_ref.at[c, rows], natural.at[c, rows], sems.at[n])
        for n, (c, rows) in enumerate(chunks)
    ]
    for load in loads:
        load.start()

    for b in range(beams):
        parent = scalars[48 + b]
        slot = lax.bitwise_xor((parent // beams) % FAMILY_DEVICES, place)
        local = parent % beams
        for k, held in enumerate((near, far)):

            @pl.when(slot % 2 == k)
            def _(held=held, local=local, slot=slot, b=b):
                for c in range(2):
                    first = pl.multiple_of((slot // 2 * 2 + c) * 512 + local * 32, 32)
                    picked[c, pl.ds(b * 32, 32)] = held[pl.ds(first, 32)]

    by_head = rows_by_head()
    for c in range(2):
        ext[c, :, 80:128] = jnp.zeros((KVH, 48, HD), jnp.bfloat16)
        for g in range(KVH):
            ext[c, g, 64:80] = new_rows[c, g * 16 : (g + 1) * 16]
        for part in range(4):
            rows = picked[c, pl.ds(part * 128, 128)]
            moved = jnp.dot(by_head, rows, preferred_element_type=jnp.float32).astype(jnp.bfloat16)
            for g in range(KVH):
                ext[c, g, pl.ds(part * 16, 16)] = moved[g * 16 : (g + 1) * 16]

    for (c, rows), load in zip(chunks, loads):
        load.wait()
        for first in range(rows.start, rows.start + step, 64):
            part = pl.ds(first, 64)
            kv[c, :, part] = jnp.swapaxes(natural[c, part], 0, 1)

    transposed = (((1,), (1,)), ((), ()))
    col = lax.broadcasted_iota(jnp.int32, (128, 128), 1)
    stats = jnp.zeros((128, 128), jnp.float32)
    for g in range(KVH):
        q = q_ref[2 * g : 2 * g + 2].reshape(128, HD)
        s = lax.dot_general(q, kv[0, g], transposed, preferred_element_type=jnp.float32)
        e = lax.dot_general(q, ext[0, g], transposed, preferred_element_type=jnp.float32)
        e = e + bias_ref[jnp.where(z == 2 * g, 1, 0)]
        m = jnp.maximum(jnp.max(s, axis=1, keepdims=True), jnp.max(e, axis=1, keepdims=True))
        p = jnp.exp2((s - m) * (scale * LOG2E))
        pe = jnp.exp2((e - m) * (scale * LOG2E))
        total = jnp.sum(p, axis=1, keepdims=True) + jnp.sum(pe, axis=1, keepdims=True)
        o = jnp.dot(p.astype(jnp.bfloat16), kv[1, g], preferred_element_type=jnp.float32)
        o = o + jnp.dot(pe.astype(jnp.bfloat16), ext[1, g], preferred_element_type=jnp.float32)
        o = (o / total).astype(jnp.bfloat16)
        out_ref[2 * g, 0:64] = o[0:64]
        out_ref[2 * g + 1, 0:64] = o[64:128]
        stats = jnp.where(col == g, m * scale + jnp.log(total), stats)
    flat = stats.T[0:KVH]
    high = flat.astype(jnp.bfloat16).astype(jnp.float32)
    middle = (flat - high).astype(jnp.bfloat16).astype(jnp.float32)
    low = flat - high - middle
    place_row = lax.broadcasted_iota(jnp.int32, (EXTRA, 128), 0)
    for g in range(KVH):
        block = jnp.where(place_row == 0, high[g : g + 1], 0.0)
        block = jnp.where(place_row == 1, middle[g : g + 1], block)
        block = jnp.where(place_row == 2, low[g : g + 1], block).astype(jnp.bfloat16)
        out_ref[2 * g, 64 : 64 + EXTRA] = block
        out_ref[2 * g + 1, 64 : 64 + EXTRA] = block


def insert_kernel(tokens_ref, parts_ref, out_ref):
    row = lax.broadcasted_iota(jnp.int32, (EXTRA, 128), 0)
    tokens = tokens_ref[0:EXTRA].astype(jnp.float32)
    for target in range(16):
        spare = parts_ref[target, 64 : 64 + EXTRA].astype(jnp.float32)
        out_ref[target, 64 : 64 + EXTRA] = jnp.where(row < 3, spare, tokens).astype(jnp.bfloat16)


def combine_kernel(scalars, parts_ref, out_ref, penalty_ref):
    z = lax.axis_index("ctx")
    extra = parts_ref[:, 64 : 64 + EXTRA].astype(jnp.float32)
    logs = extra[:, 0] + extra[:, 1] + extra[:, 2]
    weights = jnp.exp(logs - jnp.max(logs, axis=0, keepdims=True))
    weights = weights / jnp.sum(weights, axis=0, keepdims=True)
    weights = jnp.where(z % 2 == 1, pltpu.roll(weights, 64, 1), weights)
    by_row = weights.T[0:64]
    mixed = jnp.zeros((64, HD), jnp.float32)
    for source in range(16):
        mixed = mixed + by_row[:, source : source + 1] * parts_ref[source, 0:64].astype(jnp.float32)
    out_ref[...] = mixed.astype(jnp.bfloat16)

    all_tokens = extra[:, 3] * 65536.0 + extra[:, 4] * 256.0 + extra[:, 5]
    all_groups = extra[:, 6]
    used = lax.broadcasted_iota(jnp.int32, (16, 128), 1) < 32
    beam = lax.broadcasted_iota(jnp.int32, (16, 128), 0)
    counts = jnp.zeros((16, 128), jnp.float32)
    for b in range(16):
        token = scalars[b].astype(jnp.float32)
        group = scalars[16 + b].astype(jnp.float32)
        same = used & (all_tokens == token) & (all_groups < group)
        count = jnp.sum(jnp.where(same, PENALTY_WEIGHT, 0.0), axis=0, keepdims=True)
        counts = jnp.where(beam == b, count, counts)
    penalty_ref[...] = jnp.sum(counts.T, axis=0, keepdims=True)


def within_plane(block):
    pairs = [(z * 32 + b, z * 32 + (b ^ (2 * z))) for z in range(16) for b in range(32)]
    return lax.ppermute(block, ("ctx", "beam"), pairs)


def body(queries, prompt_kv, suffix_kv, new_kv, parents, lengths, token_ids, group_ids):
    vmem = pl.BlockSpec(memory_space=pltpu.VMEM)
    smem = pl.BlockSpec(memory_space=pltpu.SMEM)
    hbm = pl.BlockSpec(memory_space=pl.ANY)

    with jax.named_scope("queries_to_all"):
        sent = jnp.broadcast_to(queries.reshape(1, 64, HD), (16, 64, HD))
        everyone = lax.all_to_all(sent, "ctx", 0, 0, tiled=True)
    scalars = jnp.concatenate((token_ids, group_ids, lengths, parents))
    rows_a, rows_b = pl.pallas_call(
        token_rows_kernel,
        out_shape=(jax.ShapeDtypeStruct((2 * EXTRA, 128), jnp.bfloat16),) * 2,
        in_specs=[smem],
        out_specs=(vmem,) * 2,
        compiler_params=pltpu.CompilerParams(vmem_limit_bytes=2**20),
        name="token_rows",
    )(scalars)
    new_rows, bias = pl.pallas_call(
        prepare_kernel,
        out_shape=(
            jax.ShapeDtypeStruct((2, 128, HD), jnp.bfloat16),
            jax.ShapeDtypeStruct((2, 128, 128), jnp.float32),
        ),
        in_specs=[smem, vmem],
        out_specs=(vmem,) * 2,
        compiler_params=pltpu.CompilerParams(vmem_limit_bytes=4 * 2**20),
        name="prepare",
    )(scalars, new_kv.reshape(2, 128, HD))
    suffix = suffix_kv.reshape(1024, HD)
    with jax.named_scope("suffix_x"):
        across = lax.ppermute(suffix, "beam", [(i, i ^ 2) for i in range(32)])
    across, rows_b, new_rows, bias = lax.optimization_barrier((across, rows_b, new_rows, bias))
    with jax.named_scope("suffix_core"):
        near = jnp.concatenate((suffix, across, rows_b))
        far = lax.ppermute(near, "beam", [(i, i ^ 1) for i in range(32)])
    with jax.named_scope("tokens_plane"):
        plane = within_plane(rows_a + far[2048:])

    parts = pl.pallas_call(
        attend_kernel,
        out_shape=jax.ShapeDtypeStruct((16, 64 + EXTRA, HD), jnp.bfloat16),
        in_specs=[smem, vmem, hbm] + [vmem] * 4,
        out_specs=vmem,
        scratch_shapes=[
            pltpu.VMEM((2, 1024, KVH, HD), jnp.bfloat16),
            pltpu.VMEM((2, KVH, 1024, HD), jnp.bfloat16),
            pltpu.VMEM((2, 512, HD), jnp.bfloat16),
            pltpu.VMEM((2, KVH, 128, HD), jnp.bfloat16),
            pltpu.SemaphoreType.DMA((8,)),
        ],
        compiler_params=pltpu.CompilerParams(vmem_limit_bytes=51 * 2**20),
        cost_estimate=pl.CostEstimate(
            flops=600_000_000, bytes_accessed=6_000_000, transcendentals=1_200_000
        ),
        name="attend",
    )(scalars, everyone, prompt_kv, near, far, new_rows, bias)

    parts, plane = lax.optimization_barrier((parts, plane))
    parts = pl.pallas_call(
        insert_kernel,
        out_shape=jax.ShapeDtypeStruct(parts.shape, parts.dtype),
        in_specs=[vmem, vmem],
        out_specs=vmem,
        input_output_aliases={1: 0},
        compiler_params=pltpu.CompilerParams(vmem_limit_bytes=2 * 2**20),
        name="insert",
    )(plane, parts)
    with jax.named_scope("parts_home"):
        parts = lax.all_to_all(parts, "ctx", 0, 0, tiled=True)
    attended, penalty = pl.pallas_call(
        combine_kernel,
        out_shape=(
            jax.ShapeDtypeStruct((64, HD), jnp.bfloat16),
            jax.ShapeDtypeStruct((1, 16), jnp.float32),
        ),
        in_specs=[smem, vmem],
        out_specs=(vmem, vmem),
        compiler_params=pltpu.CompilerParams(vmem_limit_bytes=4 * 2**20),
        name="combine",
    )(scalars, parts)
    return (attended.reshape(16, 4, HD), penalty.reshape(16))


def solution(mesh):
    in_specs = (
        P("beam", "ctx", None),
        P(None, "ctx", None, None),
        P(None, "beam", "ctx", None, None),
        P(None, "beam", None, None),
        P("beam"),
        P("beam"),
        P("beam"),
        P("beam"),
    )
    out_specs = (P("beam", "ctx", None), P("beam"))
    return jax.shard_map(body, mesh=mesh, in_specs=in_specs, out_specs=out_specs, check_vma=False)
```

```python
import jax
import jax.numpy as jnp
from jax import lax
from jax.experimental import pallas as pl
from jax.experimental.pallas import tpu as pltpu
from jax.sharding import PartitionSpec as P

HEADS = 64
KVH = 8
HD = 128
FAMILY_DEVICES = 4
PENALTY_WEIGHT = 0.5
FAR_BELOW = -1e30
LOG2E = 1.4426950408889634
EXTRA = 8


def rows_by_head():
    row = lax.broadcasted_iota(jnp.int32, (128, 128), 0)
    col = lax.broadcasted_iota(jnp.int32, (128, 128), 1)
    hit = (row // 16 == col % KVH) & (row % 16 == col // KVH)
    return jnp.where(hit, 1.0, 0.0).astype(jnp.bfloat16)


def token_rows_kernel(scalars, rows_a, rows_b):
    row = lax.broadcasted_iota(jnp.int32, (EXTRA, 128), 0)
    lane = lax.broadcasted_iota(jnp.int32, (EXTRA, 128), 1)
    for rows_ref, first_lane in ((rows_a, 0), (rows_b, 16)):
        tokens = jnp.zeros((EXTRA, 128), jnp.int32)
        groups = jnp.zeros((EXTRA, 128), jnp.int32)
        for b in range(16):
            tokens = jnp.where(lane == first_lane + b, scalars[b], tokens)
            groups = jnp.where(lane == first_lane + b, scalars[16 + b], groups)
        digits = jnp.where(row == 3, tokens >> 16, 0)
        digits = jnp.where(row == 4, (tokens >> 8) & 255, digits)
        digits = jnp.where(row == 5, tokens & 255, digits)
        digits = jnp.where(row == 6, groups, digits)
        digits = jnp.concatenate((digits, jnp.zeros_like(digits)))
        rows_ref[...] = digits.astype(jnp.float32).astype(jnp.bfloat16)


def prepare_kernel(scalars, new_ref, new_rows_ref, bias_ref):
    z = lax.axis_index("ctx")
    by_head = rows_by_head()
    for c in range(2):
        moved = jnp.dot(by_head, new_ref[c], preferred_element_type=jnp.float32)
        new_rows_ref[c] = moved.astype(jnp.bfloat16)

    row = lax.broadcasted_iota(jnp.int32, (128, 128), 0)
    col = lax.broadcasted_iota(jnp.int32, (128, 128), 1)
    row_beam = (row % 64) // 4
    live = jnp.zeros((128, 128), jnp.int32)
    for b in range(16):
        live = jnp.where(row_beam == b, scalars[32 + b], live)
    on_suffix = (col < 64) & (col // 4 == row_beam) & (z * 4 + col % 4 < live)
    on_new = (col >= 64) & (col - 64 == row_beam)
    bias_ref[0] = jnp.where(on_suffix, 0.0, FAR_BELOW)
    bias_ref[1] = jnp.where(on_suffix | on_new, 0.0, FAR_BELOW)


def attend_kernel(
    scalars, q_ref, kv_ref, near, far, new_rows, bias_ref, out_ref,
    natural, kv, picked, ext, weights, sems,
):
    beams = 16
    z = lax.axis_index("ctx")
    place = lax.axis_index("beam") % FAMILY_DEVICES
    scale = HD**-0.5

    step = 256
    chunks = [(c, pl.ds(first, step)) for c in range(2) for first in range(0, 1024, step)]
    loads = [
        pltpu.make_async_copy(kv_ref.at[c, rows], natural.at[c, rows], sems.at[n])
        for n, (c, rows) in enumerate(chunks)
    ]
    for load in loads:
        load.start()

    for b in range(beams):
        parent = scalars[48 + b]
        slot = lax.bitwise_xor((parent // beams) % FAMILY_DEVICES, place)
        local = parent % beams
        for k, held in enumerate((near, far)):

            @pl.when(slot % 2 == k)
            def _(held=held, local=local, slot=slot, b=b):
                for c in range(2):
                    first = pl.multiple_of((slot // 2 * 2 + c) * 512 + local * 32, 32)
                    picked[c, pl.ds(b * 32, 32)] = held[pl.ds(first, 32)]

    by_head = rows_by_head()
    for c in range(2):
        ext[c, :, 80:128] = jnp.zeros((KVH, 48, HD), jnp.bfloat16)
        for g in range(KVH):
            ext[c, g, 64:80] = new_rows[c, g * 16 : (g + 1) * 16]
        for part in range(4):
            rows = picked[c, pl.ds(part * 128, 128)]
            moved = jnp.dot(by_head, rows, preferred_element_type=jnp.float32).astype(jnp.bfloat16)
            for g in range(KVH):
                ext[c, g, pl.ds(part * 16, 16)] = moved[g * 16 : (g + 1) * 16]

    def swap(n):
        c, rows = chunks[n]
        loads[n].wait()
        for first in range(rows.start, rows.start + step, 64):
            part = pl.ds(first, 64)
            kv[c, :, part] = jnp.swapaxes(natural[c, part], 0, 1)

    for n in range(4):
        swap(n)

    transposed = (((1,), (1,)), ((), ()))
    col = lax.broadcasted_iota(jnp.int32, (128, 128), 1)
    stats = jnp.zeros((128, 128), jnp.float32)
    def weigh(g):
        q = q_ref[2 * g : 2 * g + 2].reshape(128, HD)
        s = lax.dot_general(q, kv[0, g], transposed, preferred_element_type=jnp.float32)
        e = lax.dot_general(q, ext[0, g], transposed, preferred_element_type=jnp.float32)
        e = e + bias_ref[jnp.where(z == 2 * g, 1, 0)]
        m = jnp.maximum(jnp.max(s, axis=1, keepdims=True), jnp.max(e, axis=1, keepdims=True))
        p = jnp.exp2((s - m) * (scale * LOG2E))
        pe = jnp.exp2((e - m) * (scale * LOG2E))
        total = jnp.sum(p, axis=1, keepdims=True) + jnp.sum(pe, axis=1, keepdims=True)
        weights[g, :, 0:1024] = p.astype(jnp.bfloat16)
        weights[g, :, 1024:1152] = pe.astype(jnp.bfloat16)
        return m * scale + jnp.log(total), 1.0 / total

    def mix(g, inverse):
        o = jnp.dot(weights[g, :, 0:1024], kv[1, g], preferred_element_type=jnp.float32)
        o = o + jnp.dot(weights[g, :, 1024:1152], ext[1, g], preferred_element_type=jnp.float32)
        o = (o * inverse).astype(jnp.bfloat16)
        out_ref[2 * g, 0:64] = o[0:64]
        out_ref[2 * g + 1, 0:64] = o[64:128]

    logs, inverses = [], []
    for g in range(KVH):
        log, inverse = weigh(g)
        logs.append(log)
        inverses.append(inverse)
        if g == 1:
            for n in range(4, 8):
                swap(n)
        if g >= 2:
            mix(g - 2, inverses[g - 2])
    for g in range(6, KVH):
        mix(g, inverses[g])
    for g in range(KVH):
        stats = jnp.where(col == g, logs[g], stats)
    flat = stats.T[0:KVH]
    high = flat.astype(jnp.bfloat16).astype(jnp.float32)
    middle = (flat - high).astype(jnp.bfloat16).astype(jnp.float32)
    low = flat - high - middle
    place_row = lax.broadcasted_iota(jnp.int32, (EXTRA, 128), 0)
    for g in range(KVH):
        block = jnp.where(place_row == 0, high[g : g + 1], 0.0)
        block = jnp.where(place_row == 1, middle[g : g + 1], block)
        block = jnp.where(place_row == 2, low[g : g + 1], block).astype(jnp.bfloat16)
        out_ref[2 * g, 64 : 64 + EXTRA] = block
        out_ref[2 * g + 1, 64 : 64 + EXTRA] = block


def insert_kernel(tokens_ref, parts_ref, out_ref):
    row = lax.broadcasted_iota(jnp.int32, (EXTRA, 128), 0)
    tokens = tokens_ref[0:EXTRA].astype(jnp.float32)
    for target in range(16):
        spare = parts_ref[target, 64 : 64 + EXTRA].astype(jnp.float32)
        out_ref[target, 64 : 64 + EXTRA] = jnp.where(row < 3, spare, tokens).astype(jnp.bfloat16)


def combine_kernel(scalars, parts_ref, out_ref, penalty_ref):
    z = lax.axis_index("ctx")
    extra = parts_ref[:, 64 : 64 + EXTRA].astype(jnp.float32)
    logs = extra[:, 0] + extra[:, 1] + extra[:, 2]
    weights = jnp.exp(logs - jnp.max(logs, axis=0, keepdims=True))
    weights = weights / jnp.sum(weights, axis=0, keepdims=True)
    weights = jnp.where(z % 2 == 1, pltpu.roll(weights, 64, 1), weights)
    by_row = weights.T[0:64]
    mixed = jnp.zeros((64, HD), jnp.float32)
    for source in range(16):
        mixed = mixed + by_row[:, source : source + 1] * parts_ref[source, 0:64].astype(jnp.float32)
    out_ref[...] = mixed.astype(jnp.bfloat16)

    all_tokens = extra[:, 3] * 65536.0 + extra[:, 4] * 256.0 + extra[:, 5]
    all_groups = extra[:, 6]
    used = lax.broadcasted_iota(jnp.int32, (16, 128), 1) < 32
    beam = lax.broadcasted_iota(jnp.int32, (16, 128), 0)
    counts = jnp.zeros((16, 128), jnp.float32)
    for b in range(16):
        token = scalars[b].astype(jnp.float32)
        group = scalars[16 + b].astype(jnp.float32)
        same = used & (all_tokens == token) & (all_groups < group)
        count = jnp.sum(jnp.where(same, PENALTY_WEIGHT, 0.0), axis=0, keepdims=True)
        counts = jnp.where(beam == b, count, counts)
    penalty_ref[...] = jnp.sum(counts.T, axis=0, keepdims=True)


def within_plane(block):
    pairs = [(z * 32 + b, z * 32 + (b ^ (2 * z))) for z in range(16) for b in range(32)]
    return lax.ppermute(block, ("ctx", "beam"), pairs)


def body(queries, prompt_kv, suffix_kv, new_kv, parents, lengths, token_ids, group_ids):
    vmem = pl.BlockSpec(memory_space=pltpu.VMEM)
    smem = pl.BlockSpec(memory_space=pltpu.SMEM)
    hbm = pl.BlockSpec(memory_space=pl.ANY)

    with jax.named_scope("queries_to_all"):
        sent = jnp.broadcast_to(queries.reshape(1, 64, HD), (16, 64, HD))
        everyone = lax.all_to_all(sent, "ctx", 0, 0, tiled=True)
    scalars = jnp.concatenate((token_ids, group_ids, lengths, parents))
    rows_a, rows_b = pl.pallas_call(
        token_rows_kernel,
        out_shape=(jax.ShapeDtypeStruct((2 * EXTRA, 128), jnp.bfloat16),) * 2,
        in_specs=[smem],
        out_specs=(vmem,) * 2,
        compiler_params=pltpu.CompilerParams(vmem_limit_bytes=2**20),
        name="token_rows",
    )(scalars)
    new_rows, bias = pl.pallas_call(
        prepare_kernel,
        out_shape=(
            jax.ShapeDtypeStruct((2, 128, HD), jnp.bfloat16),
            jax.ShapeDtypeStruct((2, 128, 128), jnp.float32),
        ),
        in_specs=[smem, vmem],
        out_specs=(vmem,) * 2,
        compiler_params=pltpu.CompilerParams(vmem_limit_bytes=4 * 2**20),
        name="prepare",
    )(scalars, new_kv.reshape(2, 128, HD))
    suffix = suffix_kv.reshape(1024, HD)
    with jax.named_scope("suffix_x"):
        across = lax.ppermute(suffix, "beam", [(i, i ^ 2) for i in range(32)])
    across, rows_b, new_rows, bias = lax.optimization_barrier((across, rows_b, new_rows, bias))
    with jax.named_scope("suffix_core"):
        near = jnp.concatenate((suffix, across, rows_b))
        far = lax.ppermute(near, "beam", [(i, i ^ 1) for i in range(32)])
    with jax.named_scope("tokens_plane"):
        plane = within_plane(rows_a + far[2048:])

    parts = pl.pallas_call(
        attend_kernel,
        out_shape=jax.ShapeDtypeStruct((16, 64 + EXTRA, HD), jnp.bfloat16),
        in_specs=[smem, vmem, hbm] + [vmem] * 4,
        out_specs=vmem,
        scratch_shapes=[
            pltpu.VMEM((2, 1024, KVH, HD), jnp.bfloat16),
            pltpu.VMEM((2, KVH, 1024, HD), jnp.bfloat16),
            pltpu.VMEM((2, 512, HD), jnp.bfloat16),
            pltpu.VMEM((2, KVH, 128, HD), jnp.bfloat16),
            pltpu.VMEM((KVH, 128, 1152), jnp.bfloat16),
            pltpu.SemaphoreType.DMA((8,)),
        ],
        compiler_params=pltpu.CompilerParams(vmem_limit_bytes=51 * 2**20),
        cost_estimate=pl.CostEstimate(
            flops=600_000_000, bytes_accessed=6_000_000, transcendentals=1_200_000
        ),
        name="attend",
    )(scalars, everyone, prompt_kv, near, far, new_rows, bias)

    parts, plane = lax.optimization_barrier((parts, plane))
    parts = pl.pallas_call(
        insert_kernel,
        out_shape=jax.ShapeDtypeStruct(parts.shape, parts.dtype),
        in_specs=[vmem, vmem],
        out_specs=vmem,
        input_output_aliases={1: 0},
        compiler_params=pltpu.CompilerParams(vmem_limit_bytes=2 * 2**20),
        name="insert",
    )(plane, parts)
    with jax.named_scope("parts_home"):
        parts = lax.all_to_all(parts, "ctx", 0, 0, tiled=True)
    attended, penalty = pl.pallas_call(
        combine_kernel,
        out_shape=(
            jax.ShapeDtypeStruct((64, HD), jnp.bfloat16),
            jax.ShapeDtypeStruct((1, 16), jnp.float32),
        ),
        in_specs=[smem, vmem],
        out_specs=(vmem, vmem),
        compiler_params=pltpu.CompilerParams(vmem_limit_bytes=4 * 2**20),
        name="combine",
    )(scalars, parts)
    return (attended.reshape(16, 4, HD), penalty.reshape(16))


def solution(mesh):
    in_specs = (
        P("beam", "ctx", None),
        P(None, "ctx", None, None),
        P(None, "beam", "ctx", None, None),
        P(None, "beam", None, None),
        P("beam"),
        P("beam"),
        P("beam"),
        P("beam"),
    )
    out_specs = (P("beam", "ctx", None), P("beam"))
    return jax.shard_map(body, mesh=mesh, in_specs=in_specs, out_specs=out_specs, check_vma=False)
```

```python
import jax
import jax.numpy as jnp
from jax import lax
from jax.experimental import pallas as pl
from jax.experimental.pallas import tpu as pltpu
from jax.sharding import PartitionSpec as P

HEADS = 64
KVH = 8
HD = 128
FAMILY_DEVICES = 4
PENALTY_WEIGHT = 0.5
FAR_BELOW = -1e30
LOG2E = 1.4426950408889634
EXTRA = 8


def rows_by_head():
    row = lax.broadcasted_iota(jnp.int32, (128, 128), 0)
    col = lax.broadcasted_iota(jnp.int32, (128, 128), 1)
    hit = (row // 16 == col % KVH) & (row % 16 == col // KVH)
    return jnp.where(hit, 1.0, 0.0).astype(jnp.bfloat16)


def token_rows_kernel(scalars, rows_a, rows_b):
    row = lax.broadcasted_iota(jnp.int32, (EXTRA, 128), 0)
    lane = lax.broadcasted_iota(jnp.int32, (EXTRA, 128), 1)
    for rows_ref, first_lane in ((rows_a, 0), (rows_b, 16)):
        tokens = jnp.zeros((EXTRA, 128), jnp.int32)
        groups = jnp.zeros((EXTRA, 128), jnp.int32)
        for b in range(16):
            tokens = jnp.where(lane == first_lane + b, scalars[b], tokens)
            groups = jnp.where(lane == first_lane + b, scalars[16 + b], groups)
        digits = jnp.where(row == 3, tokens >> 16, 0)
        digits = jnp.where(row == 4, (tokens >> 8) & 255, digits)
        digits = jnp.where(row == 5, tokens & 255, digits)
        digits = jnp.where(row == 6, groups, digits)
        digits = jnp.concatenate((digits, jnp.zeros_like(digits)))
        rows_ref[...] = digits.astype(jnp.float32).astype(jnp.bfloat16)


def attend_kernel(
    scalars, q_ref, kv_ref, near, far, new_ref, out_ref,
    natural, kv, picked, ext, weights, bias_ref, sems,
):
    beams = 16
    z = lax.axis_index("ctx")
    place = lax.axis_index("beam") % FAMILY_DEVICES
    scale = HD**-0.5

    step = 256
    chunks = [(c, pl.ds(first, step)) for c in range(2) for first in range(0, 1024, step)]
    loads = [
        pltpu.make_async_copy(kv_ref.at[c, rows], natural.at[c, rows], sems.at[n])
        for n, (c, rows) in enumerate(chunks)
    ]
    for load in loads:
        load.start()

    for b in range(beams):
        parent = scalars[48 + b]
        slot = lax.bitwise_xor((parent // beams) % FAMILY_DEVICES, place)
        local = parent % beams
        for k, held in enumerate((near, far)):

            @pl.when(slot % 2 == k)
            def _(held=held, local=local, slot=slot, b=b):
                for c in range(2):
                    first = pl.multiple_of((slot // 2 * 2 + c) * 512 + local * 32, 32)
                    picked[c, pl.ds(b * 32, 32)] = held[pl.ds(first, 32)]

    by_head = rows_by_head()
    for c in range(2):
        ext[c, :, 80:128] = jnp.zeros((KVH, 48, HD), jnp.bfloat16)
        for part in range(5):
            rows = picked[c, pl.ds(part * 128, 128)] if part < 4 else new_ref[c]
            moved = jnp.dot(by_head, rows, preferred_element_type=jnp.float32).astype(jnp.bfloat16)
            for g in range(KVH):
                ext[c, g, pl.ds(part * 16, 16)] = moved[g * 16 : (g + 1) * 16]

    row = lax.broadcasted_iota(jnp.int32, (128, 128), 0)
    col = lax.broadcasted_iota(jnp.int32, (128, 128), 1)
    row_beam = (row % 64) // 4
    live = jnp.zeros((128, 128), jnp.int32)
    for b in range(16):
        live = jnp.where(row_beam == b, scalars[32 + b], live)
    on_suffix = (col < 64) & (col // 4 == row_beam) & (z * 4 + col % 4 < live)
    on_new = (col >= 64) & (col - 64 == row_beam)
    bias_ref[0] = jnp.where(on_suffix, 0.0, FAR_BELOW)
    bias_ref[1] = jnp.where(on_suffix | on_new, 0.0, FAR_BELOW)

    def swap(n):
        c, rows = chunks[n]
        loads[n].wait()
        for first in range(rows.start, rows.start + step, 64):
            part = pl.ds(first, 64)
            kv[c, :, part] = jnp.swapaxes(natural[c, part], 0, 1)

    for n in range(4):
        swap(n)

    transposed = (((1,), (1,)), ((), ()))
    stats = jnp.zeros((128, 128), jnp.float32)
    def weigh(g):
        q = q_ref[2 * g : 2 * g + 2].reshape(128, HD)
        s = lax.dot_general(q, kv[0, g], transposed, preferred_element_type=jnp.float32)
        e = lax.dot_general(q, ext[0, g], transposed, preferred_element_type=jnp.float32)
        e = e + bias_ref[jnp.where(z == 2 * g, 1, 0)]
        m = jnp.maximum(jnp.max(s, axis=1, keepdims=True), jnp.max(e, axis=1, keepdims=True))
        p = jnp.exp2((s - m) * (scale * LOG2E))
        pe = jnp.exp2((e - m) * (scale * LOG2E))
        total = jnp.sum(p, axis=1, keepdims=True) + jnp.sum(pe, axis=1, keepdims=True)
        weights[g, :, 0:1024] = p.astype(jnp.bfloat16)
        weights[g, :, 1024:1152] = pe.astype(jnp.bfloat16)
        return m * scale + jnp.log(total), 1.0 / total

    def mix(g, inverse):
        o = jnp.dot(weights[g, :, 0:1024], kv[1, g], preferred_element_type=jnp.float32)
        o = o + jnp.dot(weights[g, :, 1024:1152], ext[1, g], preferred_element_type=jnp.float32)
        o = (o * inverse).astype(jnp.bfloat16)
        out_ref[2 * g, 0:64] = o[0:64]
        out_ref[2 * g + 1, 0:64] = o[64:128]

    logs, inverses = [], []
    for g in range(KVH):
        log, inverse = weigh(g)
        logs.append(log)
        inverses.append(inverse)
        if g == 1:
            for n in range(4, 8):
                swap(n)
        if g >= 2:
            mix(g - 2, inverses[g - 2])
    for g in range(6, KVH):
        mix(g, inverses[g])
    for g in range(KVH):
        stats = jnp.where(col == g, logs[g], stats)
    flat = stats.T[0:KVH]
    high = flat.astype(jnp.bfloat16).astype(jnp.float32)
    middle = (flat - high).astype(jnp.bfloat16).astype(jnp.float32)
    low = flat - high - middle
    place_row = lax.broadcasted_iota(jnp.int32, (EXTRA, 128), 0)
    for g in range(KVH):
        block = jnp.where(place_row == 0, high[g : g + 1], 0.0)
        block = jnp.where(place_row == 1, middle[g : g + 1], block)
        block = jnp.where(place_row == 2, low[g : g + 1], block).astype(jnp.bfloat16)
        out_ref[2 * g, 64 : 64 + EXTRA] = block
        out_ref[2 * g + 1, 64 : 64 + EXTRA] = block


def insert_kernel(tokens_ref, parts_ref, out_ref):
    row = lax.broadcasted_iota(jnp.int32, (EXTRA, 128), 0)
    tokens = tokens_ref[0:EXTRA].astype(jnp.float32)
    for target in range(16):
        spare = parts_ref[target, 64 : 64 + EXTRA].astype(jnp.float32)
        out_ref[target, 64 : 64 + EXTRA] = jnp.where(row < 3, spare, tokens).astype(jnp.bfloat16)


def combine_kernel(scalars, parts_ref, out_ref, penalty_ref):
    z = lax.axis_index("ctx")
    extra = parts_ref[:, 64 : 64 + EXTRA].astype(jnp.float32)
    logs = extra[:, 0] + extra[:, 1] + extra[:, 2]
    weights = jnp.exp(logs - jnp.max(logs, axis=0, keepdims=True))
    weights = weights / jnp.sum(weights, axis=0, keepdims=True)
    weights = jnp.where(z % 2 == 1, pltpu.roll(weights, 64, 1), weights)
    by_row = weights.T[0:64]
    mixed = jnp.zeros((64, HD), jnp.float32)
    for source in range(16):
        mixed = mixed + by_row[:, source : source + 1] * parts_ref[source, 0:64].astype(jnp.float32)
    out_ref[...] = mixed.astype(jnp.bfloat16)

    all_tokens = extra[:, 3] * 65536.0 + extra[:, 4] * 256.0 + extra[:, 5]
    all_groups = extra[:, 6]
    used = lax.broadcasted_iota(jnp.int32, (16, 128), 1) < 32
    beam = lax.broadcasted_iota(jnp.int32, (16, 128), 0)
    counts = jnp.zeros((16, 128), jnp.float32)
    for b in range(16):
        token = scalars[b].astype(jnp.float32)
        group = scalars[16 + b].astype(jnp.float32)
        same = used & (all_tokens == token) & (all_groups < group)
        count = jnp.sum(jnp.where(same, PENALTY_WEIGHT, 0.0), axis=0, keepdims=True)
        counts = jnp.where(beam == b, count, counts)
    penalty_ref[...] = jnp.sum(counts.T, axis=0, keepdims=True)


def within_plane(block):
    pairs = [(z * 32 + b, z * 32 + (b ^ (2 * z))) for z in range(16) for b in range(32)]
    return lax.ppermute(block, ("ctx", "beam"), pairs)


def body(queries, prompt_kv, suffix_kv, new_kv, parents, lengths, token_ids, group_ids):
    vmem = pl.BlockSpec(memory_space=pltpu.VMEM)
    smem = pl.BlockSpec(memory_space=pltpu.SMEM)
    hbm = pl.BlockSpec(memory_space=pl.ANY)

    with jax.named_scope("queries_to_all"):
        sent = jnp.broadcast_to(queries.reshape(1, 64, HD), (16, 64, HD))
        everyone = lax.all_to_all(sent, "ctx", 0, 0, tiled=True)
    scalars = jnp.concatenate((token_ids, group_ids, lengths, parents))
    rows_a, rows_b = pl.pallas_call(
        token_rows_kernel,
        out_shape=(jax.ShapeDtypeStruct((2 * EXTRA, 128), jnp.bfloat16),) * 2,
        in_specs=[smem],
        out_specs=(vmem,) * 2,
        compiler_params=pltpu.CompilerParams(vmem_limit_bytes=2**20),
        name="token_rows",
    )(scalars)
    suffix = suffix_kv.reshape(1024, HD)
    with jax.named_scope("suffix_x"):
        across = lax.ppermute(suffix, "beam", [(i, i ^ 2) for i in range(32)])
    across, rows_b = lax.optimization_barrier((across, rows_b))
    with jax.named_scope("suffix_core"):
        near = jnp.concatenate((suffix, across, rows_b))
        far = lax.ppermute(near, "beam", [(i, i ^ 1) for i in range(32)])
    with jax.named_scope("tokens_plane"):
        plane = within_plane(rows_a + far[2048:])

    parts = pl.pallas_call(
        attend_kernel,
        out_shape=jax.ShapeDtypeStruct((16, 64 + EXTRA, HD), jnp.bfloat16),
        in_specs=[smem, vmem, hbm] + [vmem] * 3,
        out_specs=vmem,
        scratch_shapes=[
            pltpu.VMEM((2, 1024, KVH, HD), jnp.bfloat16),
            pltpu.VMEM((2, KVH, 1024, HD), jnp.bfloat16),
            pltpu.VMEM((2, 512, HD), jnp.bfloat16),
            pltpu.VMEM((2, KVH, 128, HD), jnp.bfloat16),
            pltpu.VMEM((KVH, 128, 1152), jnp.bfloat16),
            pltpu.VMEM((2, 128, 128), jnp.float32),
            pltpu.SemaphoreType.DMA((8,)),
        ],
        compiler_params=pltpu.CompilerParams(vmem_limit_bytes=51 * 2**20),
        cost_estimate=pl.CostEstimate(
            flops=600_000_000, bytes_accessed=6_000_000, transcendentals=1_200_000
        ),
        name="attend",
    )(scalars, everyone, prompt_kv, near, far, new_kv.reshape(2, 128, HD))

    parts, plane = lax.optimization_barrier((parts, plane))
    parts = pl.pallas_call(
        insert_kernel,
        out_shape=jax.ShapeDtypeStruct(parts.shape, parts.dtype),
        in_specs=[vmem, vmem],
        out_specs=vmem,
        input_output_aliases={1: 0},
        compiler_params=pltpu.CompilerParams(vmem_limit_bytes=2 * 2**20),
        name="insert",
    )(plane, parts)
    with jax.named_scope("parts_home"):
        parts = lax.all_to_all(parts, "ctx", 0, 0, tiled=True)
    attended, penalty = pl.pallas_call(
        combine_kernel,
        out_shape=(
            jax.ShapeDtypeStruct((64, HD), jnp.bfloat16),
            jax.ShapeDtypeStruct((1, 16), jnp.float32),
        ),
        in_specs=[smem, vmem],
        out_specs=(vmem, vmem),
        compiler_params=pltpu.CompilerParams(vmem_limit_bytes=4 * 2**20),
        name="combine",
    )(scalars, parts)
    return (attended.reshape(16, 4, HD), penalty.reshape(16))


def solution(mesh):
    in_specs = (
        P("beam", "ctx", None),
        P(None, "ctx", None, None),
        P(None, "beam", "ctx", None, None),
        P(None, "beam", None, None),
        P("beam"),
        P("beam"),
        P("beam"),
        P("beam"),
    )
    out_specs = (P("beam", "ctx", None), P("beam"))
    return jax.shard_map(body, mesh=mesh, in_specs=in_specs, out_specs=out_specs, check_vma=False)
```

```python
import jax
import jax.numpy as jnp
from jax import lax
from jax.experimental import pallas as pl
from jax.experimental.pallas import tpu as pltpu
from jax.sharding import PartitionSpec as P

HEADS = 64
KVH = 8
HD = 128
FAMILY_DEVICES = 4
PENALTY_WEIGHT = 0.5
FAR_BELOW = -1e30
LOG2E = 1.4426950408889634
EXTRA = 8


def rows_by_head():
    row = lax.broadcasted_iota(jnp.int32, (128, 128), 0)
    col = lax.broadcasted_iota(jnp.int32, (128, 128), 1)
    hit = (row // 16 == col % KVH) & (row % 16 == col // KVH)
    return jnp.where(hit, 1.0, 0.0).astype(jnp.bfloat16)


def token_rows_kernel(scalars, rows_ref):
    row = lax.broadcasted_iota(jnp.int32, (2 * EXTRA, 128), 0)
    lane = lax.broadcasted_iota(jnp.int32, (2 * EXTRA, 128), 1)
    tokens = jnp.zeros((2 * EXTRA, 128), jnp.int32)
    groups = jnp.zeros((2 * EXTRA, 128), jnp.int32)
    for b in range(16):
        tokens = jnp.where(lane == b, scalars[b], tokens)
        groups = jnp.where(lane == b, scalars[16 + b], groups)
    digits = jnp.where(row == 3, tokens >> 16, 0)
    digits = jnp.where(row == 4, (tokens >> 8) & 255, digits)
    digits = jnp.where(row == 5, tokens & 255, digits)
    digits = jnp.where(row == 6, groups, digits)
    rows_ref[...] = digits.astype(jnp.float32).astype(jnp.bfloat16)


def attend_kernel(
    scalars, q_ref, kv_ref, near, far, new_ref, tok_ref, out_ref,
    natural, kv, picked, ext, weights, bias_ref, sems,
):
    beams = 16
    z = lax.axis_index("ctx")
    place = lax.axis_index("beam") % FAMILY_DEVICES
    scale = HD**-0.5

    step = 256
    chunks = [(c, pl.ds(first, step)) for c in range(2) for first in range(0, 1024, step)]
    loads = [
        pltpu.make_async_copy(kv_ref.at[c, rows], natural.at[c, rows], sems.at[n])
        for n, (c, rows) in enumerate(chunks)
    ]
    for load in loads:
        load.start()

    for b in range(beams):
        parent = scalars[48 + b]
        slot = lax.bitwise_xor((parent // beams) % FAMILY_DEVICES, place)
        local = parent % beams
        for k, held in enumerate((near, far)):

            @pl.when(slot % 2 == k)
            def _(held=held, local=local, slot=slot, b=b):
                for c in range(2):
                    first = pl.multiple_of((slot // 2 * 2 + c) * 512 + local * 32, 32)
                    picked[c, pl.ds(b * 32, 32)] = held[pl.ds(first, 32)]

    by_head = rows_by_head()
    for c in range(2):
        ext[c, :, 80:128] = jnp.zeros((KVH, 48, HD), jnp.bfloat16)
        for part in range(5):
            rows = picked[c, pl.ds(part * 128, 128)] if part < 4 else new_ref[c]
            moved = jnp.dot(by_head, rows, preferred_element_type=jnp.float32).astype(jnp.bfloat16)
            for g in range(KVH):
                ext[c, g, pl.ds(part * 16, 16)] = moved[g * 16 : (g + 1) * 16]

    row = lax.broadcasted_iota(jnp.int32, (128, 128), 0)
    col = lax.broadcasted_iota(jnp.int32, (128, 128), 1)
    row_beam = (row % 64) // 4
    live = jnp.zeros((128, 128), jnp.int32)
    for b in range(16):
        live = jnp.where(row_beam == b, scalars[32 + b], live)
    on_suffix = (col < 64) & (col // 4 == row_beam) & (z * 4 + col % 4 < live)
    on_new = (col >= 64) & (col - 64 == row_beam)
    bias_ref[0] = jnp.where(on_suffix, 0.0, FAR_BELOW)
    bias_ref[1] = jnp.where(on_suffix | on_new, 0.0, FAR_BELOW)

    def swap(n):
        c, rows = chunks[n]
        loads[n].wait()
        for first in range(rows.start, rows.start + step, 64):
            part = pl.ds(first, 64)
            kv[c, :, part] = jnp.swapaxes(natural[c, part], 0, 1)

    for n in range(4):
        swap(n)

    transposed = (((1,), (1,)), ((), ()))
    stats = jnp.zeros((128, 128), jnp.float32)
    def weigh(g):
        q = q_ref[2 * g : 2 * g + 2].reshape(128, HD)
        s = lax.dot_general(q, kv[0, g], transposed, preferred_element_type=jnp.float32)
        e = lax.dot_general(q, ext[0, g], transposed, preferred_element_type=jnp.float32)
        e = e + bias_ref[jnp.where(z == 2 * g, 1, 0)]
        m = jnp.maximum(jnp.max(s, axis=1, keepdims=True), jnp.max(e, axis=1, keepdims=True))
        p = jnp.exp2((s - m) * (scale * LOG2E))
        pe = jnp.exp2((e - m) * (scale * LOG2E))
        total = jnp.sum(p, axis=1, keepdims=True) + jnp.sum(pe, axis=1, keepdims=True)
        weights[g, :, 0:1024] = p.astype(jnp.bfloat16)
        weights[g, :, 1024:1152] = pe.astype(jnp.bfloat16)
        return m * scale + jnp.log(total), 1.0 / total

    def mix(g, inverse):
        o = jnp.dot(weights[g, :, 0:1024], kv[1, g], preferred_element_type=jnp.float32)
        o = o + jnp.dot(weights[g, :, 1024:1152], ext[1, g], preferred_element_type=jnp.float32)
        o = (o * inverse).astype(jnp.bfloat16)
        out_ref[2 * g, 0:64] = o[0:64]
        out_ref[2 * g + 1, 0:64] = o[64:128]

    logs, inverses = [], []
    for g in range(KVH):
        log, inverse = weigh(g)
        logs.append(log)
        inverses.append(inverse)
        if g == 1:
            for n in range(4, 8):
                swap(n)
        if g >= 2:
            mix(g - 2, inverses[g - 2])
    for g in range(6, KVH):
        mix(g, inverses[g])
    for g in range(KVH):
        stats = jnp.where(col == g, logs[g], stats)
    flat = stats.T[0:KVH]
    high = flat.astype(jnp.bfloat16).astype(jnp.float32)
    middle = (flat - high).astype(jnp.bfloat16).astype(jnp.float32)
    low = flat - high - middle
    place_row = lax.broadcasted_iota(jnp.int32, (EXTRA, 128), 0)
    tokens = tok_ref[...].astype(jnp.float32)
    tokens = tokens + pltpu.roll(far[2048:2064].astype(jnp.float32), 16, 1)
    tokens = tokens[0:EXTRA]
    for g in range(KVH):
        block = jnp.where(place_row == 0, high[g : g + 1], tokens)
        block = jnp.where(place_row == 1, middle[g : g + 1], block)
        block = jnp.where(place_row == 2, low[g : g + 1], block).astype(jnp.bfloat16)
        out_ref[2 * g, 64 : 64 + EXTRA] = block
        out_ref[2 * g + 1, 64 : 64 + EXTRA] = block


def combine_kernel(scalars, parts_ref, out_ref, penalty_ref):
    z = lax.axis_index("ctx")
    extra = parts_ref[:, 64 : 64 + EXTRA].astype(jnp.float32)
    logs = extra[:, 0] + extra[:, 1] + extra[:, 2]
    weights = jnp.exp(logs - jnp.max(logs, axis=0, keepdims=True))
    weights = weights / jnp.sum(weights, axis=0, keepdims=True)
    weights = jnp.where(z % 2 == 1, pltpu.roll(weights, 64, 1), weights)
    by_row = weights.T[0:64]
    mixed = jnp.zeros((64, HD), jnp.float32)
    for source in range(16):
        mixed = mixed + by_row[:, source : source + 1] * parts_ref[source, 0:64].astype(jnp.float32)
    out_ref[...] = mixed.astype(jnp.bfloat16)

    all_tokens = extra[:, 3] * 65536.0 + extra[:, 4] * 256.0 + extra[:, 5]
    all_groups = extra[:, 6]
    used = lax.broadcasted_iota(jnp.int32, (16, 128), 1) < 32
    beam = lax.broadcasted_iota(jnp.int32, (16, 128), 0)
    counts = jnp.zeros((16, 128), jnp.float32)
    for b in range(16):
        token = scalars[b].astype(jnp.float32)
        group = scalars[16 + b].astype(jnp.float32)
        same = used & (all_tokens == token) & (all_groups < group)
        count = jnp.sum(jnp.where(same, PENALTY_WEIGHT, 0.0), axis=0, keepdims=True)
        counts = jnp.where(beam == b, count, counts)
    penalty_ref[...] = jnp.sum(counts.T, axis=0, keepdims=True)


TOKENS_FROM = (10, 9, 11, 6, 15, 7, 5, 12, 0, 1, 3, 4, 13, 8, 2, 14)


def within_plane(block):
    pairs = [(z * 32 + b, z * 32 + (b ^ (2 * TOKENS_FROM[z]))) for z in range(16) for b in range(32)]
    return lax.ppermute(block, ("ctx", "beam"), pairs)


def body(queries, prompt_kv, suffix_kv, new_kv, parents, lengths, token_ids, group_ids):
    vmem = pl.BlockSpec(memory_space=pltpu.VMEM)
    smem = pl.BlockSpec(memory_space=pltpu.SMEM)
    hbm = pl.BlockSpec(memory_space=pl.ANY)

    with jax.named_scope("queries_to_all"):
        sent = jnp.broadcast_to(queries.reshape(1, 64, HD), (16, 64, HD))
        everyone = lax.all_to_all(sent, "ctx", 0, 0, tiled=True)
    scalars = jnp.concatenate((token_ids, group_ids, lengths, parents))
    rows = pl.pallas_call(
        token_rows_kernel,
        out_shape=jax.ShapeDtypeStruct((2 * EXTRA, 128), jnp.bfloat16),
        in_specs=[smem],
        out_specs=vmem,
        compiler_params=pltpu.CompilerParams(vmem_limit_bytes=2**20),
        cost_estimate=pl.CostEstimate(
            flops=30_000_000_000, bytes_accessed=1_000_000, transcendentals=0
        ),
        name="token_rows",
    )(scalars)
    suffix = suffix_kv.reshape(1024, HD)
    with jax.named_scope("suffix_x"):
        across = lax.ppermute(suffix, "beam", [(i, i ^ 2) for i in range(32)])
    with jax.named_scope("tokens_plane"):
        tokens = within_plane(rows)
    across, tokens = lax.optimization_barrier((across, tokens))
    with jax.named_scope("suffix_core"):
        near = jnp.concatenate((suffix, across, tokens))
        far = lax.ppermute(near, "beam", [(i, i ^ 1) for i in range(32)])

    parts = pl.pallas_call(
        attend_kernel,
        out_shape=jax.ShapeDtypeStruct((16, 64 + EXTRA, HD), jnp.bfloat16),
        in_specs=[smem, vmem, hbm] + [vmem] * 4,
        out_specs=vmem,
        scratch_shapes=[
            pltpu.VMEM((2, 1024, KVH, HD), jnp.bfloat16),
            pltpu.VMEM((2, KVH, 1024, HD), jnp.bfloat16),
            pltpu.VMEM((2, 512, HD), jnp.bfloat16),
            pltpu.VMEM((2, KVH, 128, HD), jnp.bfloat16),
            pltpu.VMEM((KVH, 128, 1152), jnp.bfloat16),
            pltpu.VMEM((2, 128, 128), jnp.float32),
            pltpu.SemaphoreType.DMA((8,)),
        ],
        compiler_params=pltpu.CompilerParams(vmem_limit_bytes=51 * 2**20),
        cost_estimate=pl.CostEstimate(
            flops=600_000_000, bytes_accessed=6_000_000, transcendentals=1_200_000
        ),
        name="attend",
    )(scalars, everyone, prompt_kv, near, far, new_kv.reshape(2, 128, HD), tokens)

    with jax.named_scope("parts_home"):
        parts = lax.all_to_all(parts, "ctx", 0, 0, tiled=True)
    attended, penalty = pl.pallas_call(
        combine_kernel,
        out_shape=(
            jax.ShapeDtypeStruct((64, HD), jnp.bfloat16),
            jax.ShapeDtypeStruct((1, 16), jnp.float32),
        ),
        in_specs=[smem, vmem],
        out_specs=(vmem, vmem),
        compiler_params=pltpu.CompilerParams(vmem_limit_bytes=4 * 2**20),
        name="combine",
    )(scalars, parts)
    return (attended.reshape(16, 4, HD), penalty.reshape(16))


def solution(mesh):
    in_specs = (
        P("beam", "ctx", None),
        P(None, "ctx", None, None),
        P(None, "beam", "ctx", None, None),
        P(None, "beam", None, None),
        P("beam"),
        P("beam"),
        P("beam"),
        P("beam"),
    )
    out_specs = (P("beam", "ctx", None), P("beam"))
    return jax.shard_map(body, mesh=mesh, in_specs=in_specs, out_specs=out_specs, check_vma=False)
```

```python
import jax
import jax.numpy as jnp
from jax import lax
from jax.experimental import pallas as pl
from jax.experimental.pallas import tpu as pltpu
from jax.sharding import PartitionSpec as P

HEADS = 64
KVH = 8
HD = 128
FAMILY_DEVICES = 4
PENALTY_WEIGHT = 0.5
FAR_BELOW = -1e30
LOG2E = 1.4426950408889634
EXTRA = 8


def rows_by_head():
    row = lax.broadcasted_iota(jnp.int32, (128, 128), 0)
    col = lax.broadcasted_iota(jnp.int32, (128, 128), 1)
    hit = (row // 16 == col % KVH) & (row % 16 == col // KVH)
    return jnp.where(hit, 1.0, 0.0).astype(jnp.bfloat16)


def token_rows_kernel(scalars, rows_ref):
    row = lax.broadcasted_iota(jnp.int32, (2 * EXTRA, 128), 0)
    lane = lax.broadcasted_iota(jnp.int32, (2 * EXTRA, 128), 1)
    tokens = jnp.zeros((2 * EXTRA, 128), jnp.int32)
    groups = jnp.zeros((2 * EXTRA, 128), jnp.int32)
    for b in range(16):
        tokens = jnp.where(lane == b, scalars[b], tokens)
        groups = jnp.where(lane == b, scalars[16 + b], groups)
    digits = jnp.where(row == 3, tokens >> 16, 0)
    digits = jnp.where(row == 4, (tokens >> 8) & 255, digits)
    digits = jnp.where(row == 5, tokens & 255, digits)
    digits = jnp.where(row == 6, groups, digits)
    rows_ref[...] = digits.astype(jnp.float32).astype(jnp.bfloat16)


def attend_kernel(
    scalars, q_ref, kv_ref, near, far, new_ref, tok_ref, out_ref,
    natural, kv, picked, ext, weights, bias_ref, sems,
):
    beams = 16
    z = lax.axis_index("ctx")
    place = lax.axis_index("beam") % FAMILY_DEVICES
    scale = HD**-0.5

    step = 256
    chunks = [(c, pl.ds(first, step)) for c in range(2) for first in range(0, 1024, step)]
    loads = [
        pltpu.make_async_copy(kv_ref.at[c, rows], natural.at[c, rows], sems.at[n])
        for n, (c, rows) in enumerate(chunks)
    ]
    for load in loads:
        load.start()

    for b in range(beams):
        parent = scalars[48 + b]
        slot = lax.bitwise_xor((parent // beams) % FAMILY_DEVICES, place)
        local = parent % beams
        for k, held in enumerate((near, far)):

            @pl.when(slot % 2 == k)
            def _(held=held, local=local, slot=slot, b=b):
                for c in range(2):
                    first = pl.multiple_of((slot // 2 * 2 + c) * 512 + local * 32, 32)
                    picked[c, pl.ds(b * 32, 32)] = held[pl.ds(first, 32)]

    by_head = rows_by_head()
    for c in range(2):
        ext[c, :, 80:128] = jnp.zeros((KVH, 48, HD), jnp.bfloat16)
        for part in range(5):
            rows = picked[c, pl.ds(part * 128, 128)] if part < 4 else new_ref[c]
            moved = jnp.dot(by_head, rows, preferred_element_type=jnp.float32).astype(jnp.bfloat16)
            for g in range(KVH):
                ext[c, g, pl.ds(part * 16, 16)] = moved[g * 16 : (g + 1) * 16]

    row = lax.broadcasted_iota(jnp.int32, (128, 128), 0)
    col = lax.broadcasted_iota(jnp.int32, (128, 128), 1)
    row_beam = (row % 64) // 4
    live = jnp.zeros((128, 128), jnp.int32)
    for b in range(16):
        live = jnp.where(row_beam == b, scalars[32 + b], live)
    on_suffix = (col < 64) & (col // 4 == row_beam) & (z * 4 + col % 4 < live)
    on_new = (col >= 64) & (col - 64 == row_beam)
    bias_ref[0] = jnp.where(on_suffix, 0.0, FAR_BELOW)
    bias_ref[1] = jnp.where(on_suffix | on_new, 0.0, FAR_BELOW)

    def swap(n):
        c, rows = chunks[n]
        loads[n].wait()
        for first in range(rows.start, rows.start + step, 64):
            part = pl.ds(first, 64)
            kv[c, :, part] = jnp.swapaxes(natural[c, part], 0, 1)

    for n in range(4):
        swap(n)

    transposed = (((1,), (1,)), ((), ()))
    stats = jnp.zeros((128, 128), jnp.float32)
    def weigh(g):
        q = q_ref[2 * g : 2 * g + 2].reshape(128, HD)
        s = lax.dot_general(q, kv[0, g], transposed, preferred_element_type=jnp.float32)
        e = lax.dot_general(q, ext[0, g], transposed, preferred_element_type=jnp.float32)
        e = e + bias_ref[jnp.where(z == 2 * g, 1, 0)]
        m = jnp.maximum(jnp.max(s, axis=1, keepdims=True), jnp.max(e, axis=1, keepdims=True))
        p = jnp.exp2((s - m) * (scale * LOG2E))
        pe = jnp.exp2((e - m) * (scale * LOG2E))
        total = jnp.sum(p, axis=1, keepdims=True) + jnp.sum(pe, axis=1, keepdims=True)
        weights[g, :, 0:1024] = p.astype(jnp.bfloat16)
        weights[g, :, 1024:1152] = pe.astype(jnp.bfloat16)
        return m * scale + jnp.log(total), 1.0 / total

    def mix(g, inverse):
        o = jnp.dot(weights[g, :, 0:1024], kv[1, g], preferred_element_type=jnp.float32)
        o = o + jnp.dot(weights[g, :, 1024:1152], ext[1, g], preferred_element_type=jnp.float32)
        o = (o * inverse).astype(jnp.bfloat16)
        out_ref[2 * g, 0:64] = o[0:64]
        out_ref[2 * g + 1, 0:64] = o[64:128]

    logs, inverses = [], []
    for g in range(KVH):
        log, inverse = weigh(g)
        logs.append(log)
        inverses.append(inverse)
        if g == 1:
            for n in range(4, 8):
                swap(n)
        if g >= 2:
            mix(g - 2, inverses[g - 2])
    for g in range(6, KVH):
        mix(g, inverses[g])
    for g in range(KVH):
        stats = jnp.where(col == g, logs[g], stats)
    flat = stats.T[0:KVH]
    high = flat.astype(jnp.bfloat16).astype(jnp.float32)
    middle = (flat - high).astype(jnp.bfloat16).astype(jnp.float32)
    low = flat - high - middle
    place_row = lax.broadcasted_iota(jnp.int32, (EXTRA, 128), 0)
    tokens = tok_ref[...].astype(jnp.float32)
    tokens = tokens + pltpu.roll(far[2048:2064].astype(jnp.float32), 16, 1)
    tokens = tokens[0:EXTRA]
    for g in range(KVH):
        block = jnp.where(place_row == 0, high[g : g + 1], tokens)
        block = jnp.where(place_row == 1, middle[g : g + 1], block)
        block = jnp.where(place_row == 2, low[g : g + 1], block).astype(jnp.bfloat16)
        out_ref[2 * g, 64 : 64 + EXTRA] = block
        out_ref[2 * g + 1, 64 : 64 + EXTRA] = block


def combine_kernel(scalars, parts_ref, out_ref, penalty_ref):
    z = lax.axis_index("ctx")
    extra = parts_ref[:, 64 : 64 + EXTRA].astype(jnp.float32)
    logs = extra[:, 0] + extra[:, 1] + extra[:, 2]
    weights = jnp.exp(logs - jnp.max(logs, axis=0, keepdims=True))
    weights = weights * (1.0 / jnp.sum(weights, axis=0, keepdims=True))
    weights = jnp.where(z % 2 == 1, pltpu.roll(weights, 64, 1), weights)
    by_row = weights.T[0:64]
    mixed = jnp.zeros((64, HD), jnp.float32)
    for source in range(16):
        mixed = mixed + by_row[:, source : source + 1] * parts_ref[source, 0:64].astype(jnp.float32)
    out_ref[...] = mixed.astype(jnp.bfloat16)

    all_tokens = extra[:, 3] * 65536.0 + extra[:, 4] * 256.0 + extra[:, 5]
    all_groups = extra[:, 6]
    used = lax.broadcasted_iota(jnp.int32, (16, 128), 1) < 32
    all_groups = jnp.where(used, all_groups, 1e9)
    lane = lax.broadcasted_iota(jnp.int32, (1, 128), 1)
    counts = jnp.zeros((1, 128), jnp.float32)
    for b in range(16):
        token = scalars[b].astype(jnp.float32)
        group = scalars[16 + b].astype(jnp.float32)
        same = (all_tokens == token) & (all_groups < group)
        count = jnp.sum(jnp.where(same, PENALTY_WEIGHT, 0.0))
        counts = jnp.where(lane == b, count, counts)
    penalty_ref[...] = counts[:, 0:16]


TOKENS_FROM = (10, 9, 11, 6, 15, 7, 5, 12, 0, 1, 3, 4, 13, 8, 2, 14)


def within_plane(block):
    pairs = [(z * 32 + b, z * 32 + (b ^ (2 * TOKENS_FROM[z]))) for z in range(16) for b in range(32)]
    return lax.ppermute(block, ("ctx", "beam"), pairs)


def body(queries, prompt_kv, suffix_kv, new_kv, parents, lengths, token_ids, group_ids):
    vmem = pl.BlockSpec(memory_space=pltpu.VMEM)
    smem = pl.BlockSpec(memory_space=pltpu.SMEM)
    hbm = pl.BlockSpec(memory_space=pl.ANY)

    with jax.named_scope("queries_to_all"):
        sent = jnp.broadcast_to(queries.reshape(1, 64, HD), (16, 64, HD))
        everyone = lax.all_to_all(sent, "ctx", 0, 0, tiled=True)
    scalars = jnp.concatenate((token_ids, group_ids, lengths, parents))
    rows = pl.pallas_call(
        token_rows_kernel,
        out_shape=jax.ShapeDtypeStruct((2 * EXTRA, 128), jnp.bfloat16),
        in_specs=[smem],
        out_specs=vmem,
        compiler_params=pltpu.CompilerParams(vmem_limit_bytes=2**20),
        cost_estimate=pl.CostEstimate(
            flops=30_000_000_000, bytes_accessed=1_000_000, transcendentals=0
        ),
        name="token_rows",
    )(scalars)
    suffix = suffix_kv.reshape(1024, HD)
    with jax.named_scope("suffix_x"):
        across = lax.ppermute(suffix, "beam", [(i, i ^ 2) for i in range(32)])
    with jax.named_scope("tokens_plane"):
        tokens = within_plane(rows)
    across, tokens = lax.optimization_barrier((across, tokens))
    with jax.named_scope("suffix_core"):
        near = jnp.concatenate((suffix, across, tokens))
        far = lax.ppermute(near, "beam", [(i, i ^ 1) for i in range(32)])

    parts = pl.pallas_call(
        attend_kernel,
        out_shape=jax.ShapeDtypeStruct((16, 64 + EXTRA, HD), jnp.bfloat16),
        in_specs=[smem, vmem, hbm] + [vmem] * 4,
        out_specs=vmem,
        scratch_shapes=[
            pltpu.VMEM((2, 1024, KVH, HD), jnp.bfloat16),
            pltpu.VMEM((2, KVH, 1024, HD), jnp.bfloat16),
            pltpu.VMEM((2, 512, HD), jnp.bfloat16),
            pltpu.VMEM((2, KVH, 128, HD), jnp.bfloat16),
            pltpu.VMEM((KVH, 128, 1152), jnp.bfloat16),
            pltpu.VMEM((2, 128, 128), jnp.float32),
            pltpu.SemaphoreType.DMA((8,)),
        ],
        compiler_params=pltpu.CompilerParams(vmem_limit_bytes=51 * 2**20),
        cost_estimate=pl.CostEstimate(
            flops=600_000_000, bytes_accessed=6_000_000, transcendentals=1_200_000
        ),
        name="attend",
    )(scalars, everyone, prompt_kv, near, far, new_kv.reshape(2, 128, HD), tokens)

    with jax.named_scope("parts_home"):
        parts = lax.all_to_all(parts, "ctx", 0, 0, tiled=True)
    attended, penalty = pl.pallas_call(
        combine_kernel,
        out_shape=(
            jax.ShapeDtypeStruct((64, HD), jnp.bfloat16),
            jax.ShapeDtypeStruct((1, 16), jnp.float32),
        ),
        in_specs=[smem, vmem],
        out_specs=(vmem, vmem),
        compiler_params=pltpu.CompilerParams(vmem_limit_bytes=4 * 2**20),
        name="combine",
    )(scalars, parts)
    return (attended.reshape(16, 4, HD), penalty.reshape(16))


def solution(mesh):
    in_specs = (
        P("beam", "ctx", None),
        P(None, "ctx", None, None),
        P(None, "beam", "ctx", None, None),
        P(None, "beam", None, None),
        P("beam"),
        P("beam"),
        P("beam"),
        P("beam"),
    )
    out_specs = (P("beam", "ctx", None), P("beam"))
    return jax.shard_map(body, mesh=mesh, in_specs=in_specs, out_specs=out_specs, check_vma=False)
```

```python
import jax
import jax.numpy as jnp
from jax import lax
from jax.experimental import pallas as pl
from jax.experimental.pallas import tpu as pltpu
from jax.sharding import PartitionSpec as P

HEADS = 64
KVH = 8
HD = 128
FAMILY_DEVICES = 4
PENALTY_WEIGHT = 0.5
FAR_BELOW = -1e30
LOG2E = 1.4426950408889634
EXTRA = 8


def rows_by_head():
    row = lax.broadcasted_iota(jnp.int32, (128, 128), 0)
    col = lax.broadcasted_iota(jnp.int32, (128, 128), 1)
    hit = (row // 16 == col % KVH) & (row % 16 == col // KVH)
    return jnp.where(hit, 1.0, 0.0).astype(jnp.bfloat16)


def token_rows_kernel(scalars, rows_ref):
    row = lax.broadcasted_iota(jnp.int32, (2 * EXTRA, 128), 0)
    lane = lax.broadcasted_iota(jnp.int32, (2 * EXTRA, 128), 1)
    tokens = jnp.zeros((2 * EXTRA, 128), jnp.int32)
    groups = jnp.zeros((2 * EXTRA, 128), jnp.int32)
    for b in range(16):
        tokens = jnp.where(lane == b, scalars[b], tokens)
        groups = jnp.where(lane == b, scalars[16 + b], groups)
    digits = jnp.where(row == 3, tokens >> 16, 0)
    digits = jnp.where(row == 4, (tokens >> 8) & 255, digits)
    digits = jnp.where(row == 5, tokens & 255, digits)
    digits = jnp.where(row == 6, groups, digits)
    rows_ref[...] = digits.astype(jnp.float32).astype(jnp.bfloat16)


def attend_kernel(
    scalars, q_ref, kv_ref, near, far, new_ref, tok_ref, out_ref,
    natural, kv, picked, ext, weights, bias_ref, sems,
):
    beams = 16
    z = lax.axis_index("ctx")
    place = lax.axis_index("beam") % FAMILY_DEVICES
    scale = HD**-0.5

    step = 256
    chunks = [(c, pl.ds(first, step)) for c in range(2) for first in range(0, 1024, step)]
    loads = [
        pltpu.make_async_copy(kv_ref.at[c, rows], natural.at[c, rows], sems.at[n])
        for n, (c, rows) in enumerate(chunks)
    ]
    for load in loads:
        load.start()

    for b in range(beams):
        parent = scalars[48 + b]
        slot = lax.bitwise_xor((parent // beams) % FAMILY_DEVICES, place)
        local = parent % beams
        for k, held in enumerate((near, far)):

            @pl.when(slot % 2 == k)
            def _(held=held, local=local, slot=slot, b=b):
                for c in range(2):
                    first = pl.multiple_of((slot // 2 * 2 + c) * 512 + local * 32, 32)
                    picked[c, pl.ds(b * 32, 32)] = held[pl.ds(first, 32)]

    by_head = rows_by_head()
    for c in range(2):
        ext[c, :, 80:128] = jnp.zeros((KVH, 48, HD), jnp.bfloat16)
        for part in range(5):
            rows = picked[c, pl.ds(part * 128, 128)] if part < 4 else new_ref[c]
            moved = jnp.dot(by_head, rows, preferred_element_type=jnp.float32).astype(jnp.bfloat16)
            for g in range(KVH):
                ext[c, g, pl.ds(part * 16, 16)] = moved[g * 16 : (g + 1) * 16]

    row = lax.broadcasted_iota(jnp.int32, (128, 128), 0)
    col = lax.broadcasted_iota(jnp.int32, (128, 128), 1)
    row_beam = (row % 64) // 4
    live = jnp.zeros((128, 128), jnp.int32)
    for b in range(16):
        live = jnp.where(row_beam == b, scalars[32 + b], live)
    on_suffix = (col < 64) & (col // 4 == row_beam) & (z * 4 + col % 4 < live)
    on_new = (col >= 64) & (col - 64 == row_beam)
    bias_ref[0] = jnp.where(on_suffix, 0.0, FAR_BELOW)
    bias_ref[1] = jnp.where(on_suffix | on_new, 0.0, FAR_BELOW)

    def swap(n):
        c, rows = chunks[n]
        loads[n].wait()
        for first in range(rows.start, rows.start + step, 64):
            part = pl.ds(first, 64)
            kv[c, :, part] = jnp.swapaxes(natural[c, part], 0, 1)

    for n in range(4):
        swap(n)

    transposed = (((1,), (1,)), ((), ()))
    stats = jnp.zeros((128, 128), jnp.float32)
    def weigh(g):
        q = q_ref[2 * g : 2 * g + 2].reshape(128, HD)
        s = lax.dot_general(q, kv[0, g], transposed, preferred_element_type=jnp.float32)
        e = lax.dot_general(q, ext[0, g], transposed, preferred_element_type=jnp.float32)
        e = e + bias_ref[jnp.where(z == 2 * g, 1, 0)]
        m = jnp.maximum(jnp.max(s, axis=1, keepdims=True), jnp.max(e, axis=1, keepdims=True))
        p = jnp.exp2((s - m) * (scale * LOG2E))
        pe = jnp.exp2((e - m) * (scale * LOG2E))
        total = jnp.sum(p, axis=1, keepdims=True) + jnp.sum(pe, axis=1, keepdims=True)
        weights[g, :, 0:1024] = p.astype(jnp.bfloat16)
        weights[g, :, 1024:1152] = pe.astype(jnp.bfloat16)
        return m * scale + jnp.log(total), 1.0 / total

    def mix(g, inverse):
        o = jnp.dot(weights[g, :, 0:1024], kv[1, g], preferred_element_type=jnp.float32)
        o = o + jnp.dot(weights[g, :, 1024:1152], ext[1, g], preferred_element_type=jnp.float32)
        o = (o * inverse).astype(jnp.bfloat16)
        out_ref[2 * g, 0:64] = o[0:64]
        out_ref[2 * g + 1, 0:64] = o[64:128]

    logs, inverses = [], []
    for g in range(KVH):
        log, inverse = weigh(g)
        logs.append(log)
        inverses.append(inverse)
        if g == 1:
            for n in range(4, 8):
                swap(n)
        if g >= 2:
            mix(g - 2, inverses[g - 2])
    for g in range(6, KVH):
        mix(g, inverses[g])
    for g in range(KVH):
        stats = jnp.where(col == g, logs[g], stats)
    flat = stats.T[0:KVH]
    high = flat.astype(jnp.bfloat16).astype(jnp.float32)
    middle = (flat - high).astype(jnp.bfloat16).astype(jnp.float32)
    low = flat - high - middle
    place_row = lax.broadcasted_iota(jnp.int32, (EXTRA, 128), 0)
    tokens = tok_ref[...].astype(jnp.float32)
    tokens = tokens + pltpu.roll(far[2048:2064].astype(jnp.float32), 16, 1)
    tokens = tokens[0:EXTRA]
    for g in range(KVH):
        block = jnp.where(place_row == 0, high[g : g + 1], tokens)
        block = jnp.where(place_row == 1, middle[g : g + 1], block)
        block = jnp.where(place_row == 2, low[g : g + 1], block).astype(jnp.bfloat16)
        out_ref[2 * g, 64 : 64 + EXTRA] = block
        out_ref[2 * g + 1, 64 : 64 + EXTRA] = block


def combine_kernel(scalars, parts_ref, out_ref, penalty_ref):
    z = lax.axis_index("ctx")
    extra = parts_ref[:, 64 : 64 + EXTRA].astype(jnp.float32)
    logs = extra[:, 0] + extra[:, 1] + extra[:, 2]
    weights = jnp.exp(logs - jnp.max(logs, axis=0, keepdims=True))
    weights = weights * (1.0 / jnp.sum(weights, axis=0, keepdims=True))
    weights = jnp.where(z % 2 == 1, pltpu.roll(weights, 64, 1), weights)
    by_row = weights.T[0:64]
    halves = []
    for first in (0, 8):
        half = jnp.zeros((64, HD), jnp.float32)
        for source in range(first, first + 8):
            part = parts_ref[source, 0:64].astype(jnp.float32)
            half = half + by_row[:, source : source + 1] * part
        halves.append(half)
    mixed = halves[0] + halves[1]
    out_ref[...] = mixed.astype(jnp.bfloat16)

    all_tokens = extra[:, 3] * 65536.0 + extra[:, 4] * 256.0 + extra[:, 5]
    all_groups = extra[:, 6]
    used = lax.broadcasted_iota(jnp.int32, (16, 128), 1) < 32
    all_groups = jnp.where(used, all_groups, 1e9)
    lane = lax.broadcasted_iota(jnp.int32, (1, 128), 1)
    counts = jnp.zeros((1, 128), jnp.float32)
    for b in range(16):
        token = scalars[b].astype(jnp.float32)
        group = scalars[16 + b].astype(jnp.float32)
        same = (all_tokens == token) & (all_groups < group)
        count = jnp.sum(jnp.where(same, PENALTY_WEIGHT, 0.0))
        counts = jnp.where(lane == b, count, counts)
    penalty_ref[...] = counts[:, 0:16]


TOKENS_FROM = (10, 9, 11, 6, 15, 7, 5, 12, 0, 1, 3, 4, 13, 8, 2, 14)


def within_plane(block):
    pairs = [(z * 32 + b, z * 32 + (b ^ (2 * TOKENS_FROM[z]))) for z in range(16) for b in range(32)]
    return lax.ppermute(block, ("ctx", "beam"), pairs)


def body(queries, prompt_kv, suffix_kv, new_kv, parents, lengths, token_ids, group_ids):
    vmem = pl.BlockSpec(memory_space=pltpu.VMEM)
    smem = pl.BlockSpec(memory_space=pltpu.SMEM)
    hbm = pl.BlockSpec(memory_space=pl.ANY)

    with jax.named_scope("queries_to_all"):
        sent = jnp.broadcast_to(queries.reshape(1, 64, HD), (16, 64, HD))
        everyone = lax.all_to_all(sent, "ctx", 0, 0, tiled=True)
    scalars = jnp.concatenate((token_ids, group_ids, lengths, parents))
    rows = pl.pallas_call(
        token_rows_kernel,
        out_shape=jax.ShapeDtypeStruct((2 * EXTRA, 128), jnp.bfloat16),
        in_specs=[smem],
        out_specs=vmem,
        compiler_params=pltpu.CompilerParams(vmem_limit_bytes=2**20),
        cost_estimate=pl.CostEstimate(
            flops=30_000_000_000, bytes_accessed=1_000_000, transcendentals=0
        ),
        name="token_rows",
    )(scalars)
    suffix = suffix_kv.reshape(1024, HD)
    with jax.named_scope("suffix_x"):
        across = lax.ppermute(suffix, "beam", [(i, i ^ 2) for i in range(32)])
    with jax.named_scope("tokens_plane"):
        tokens = within_plane(rows)
    across, tokens = lax.optimization_barrier((across, tokens))
    with jax.named_scope("suffix_core"):
        near = jnp.concatenate((suffix, across, tokens))
        far = lax.ppermute(near, "beam", [(i, i ^ 1) for i in range(32)])

    parts = pl.pallas_call(
        attend_kernel,
        out_shape=jax.ShapeDtypeStruct((16, 64 + EXTRA, HD), jnp.bfloat16),
        in_specs=[smem, vmem, hbm] + [vmem] * 4,
        out_specs=vmem,
        scratch_shapes=[
            pltpu.VMEM((2, 1024, KVH, HD), jnp.bfloat16),
            pltpu.VMEM((2, KVH, 1024, HD), jnp.bfloat16),
            pltpu.VMEM((2, 512, HD), jnp.bfloat16),
            pltpu.VMEM((2, KVH, 128, HD), jnp.bfloat16),
            pltpu.VMEM((KVH, 128, 1152), jnp.bfloat16),
            pltpu.VMEM((2, 128, 128), jnp.float32),
            pltpu.SemaphoreType.DMA((8,)),
        ],
        compiler_params=pltpu.CompilerParams(vmem_limit_bytes=51 * 2**20),
        cost_estimate=pl.CostEstimate(
            flops=600_000_000, bytes_accessed=6_000_000, transcendentals=1_200_000
        ),
        name="attend",
    )(scalars, everyone, prompt_kv, near, far, new_kv.reshape(2, 128, HD), tokens)

    with jax.named_scope("parts_home"):
        parts = lax.all_to_all(parts, "ctx", 0, 0, tiled=True)
    attended, penalty = pl.pallas_call(
        combine_kernel,
        out_shape=(
            jax.ShapeDtypeStruct((64, HD), jnp.bfloat16),
            jax.ShapeDtypeStruct((1, 16), jnp.float32),
        ),
        in_specs=[smem, vmem],
        out_specs=(vmem, vmem),
        compiler_params=pltpu.CompilerParams(vmem_limit_bytes=4 * 2**20),
        name="combine",
    )(scalars, parts)
    return (attended.reshape(16, 4, HD), penalty.reshape(16))


def solution(mesh):
    in_specs = (
        P("beam", "ctx", None),
        P(None, "ctx", None, None),
        P(None, "beam", "ctx", None, None),
        P(None, "beam", None, None),
        P("beam"),
        P("beam"),
        P("beam"),
        P("beam"),
    )
    out_specs = (P("beam", "ctx", None), P("beam"))
    return jax.shard_map(body, mesh=mesh, in_specs=in_specs, out_specs=out_specs, check_vma=False)
```
